512 devices in a mesh: rows: 32 (over z, core), vocab: 16 (over x, y).
Axes of the slice: x: 4, y: 4, z: 16, core: 2. Of those that a mesh axis runs over, the one named last changes fastest.
Arguments:
- student_hidden: bfloat16 [192, 5120], P('rows', 'vocab'), may hold values from -12 to 12
- teacher_hidden: bfloat16 [192, 4096], P('rows', 'vocab'), may hold values from -12 to 12
- student_head: bfloat16 [5120, 143360], P(None, ('rows', 'vocab')), may hold values from -0.13975425 to 0.13975425
- teacher_head: bfloat16 [4096, 143360], P(None, ('rows', 'vocab')), may hold values from -0.15625 to 0.15625
- teacher_row: int32 [192], replicated, may hold values from 0 to 191, each once
- live_counts: int32 [32], replicated, may hold values from 1 to 6, 112 in all
- branch_id: int32 [192], replicated, may hold values from 0 to 15
- branch_ratio: float32 [16], replicated, may hold values from 0.25 to 4
Outputs:
- token_loss: float32 [192], P('rows')
- grad_hidden: float32 [192, 5120], P('rows', 'vocab')
The draws below stay inside these ranges and needn't reach their ends.
Inputs may be any that keep to these rules, and one draw needn't show every extreme that they name: `live_counts`: the counts sum to 112.
All inputs are finite; a program needn't handle non-finite values.
Results may differ from the reference program's by a relative error of at most 0.0045.
Values may be sent and summed in bfloat16 or wider, within the bound.
A program may use at most 64 MiB of HBM per device.

```python
import math
import jax
import jax.numpy as jnp
import numpy as np

DS = 5120
DT = 4096
TOK_DEV = 6
NBR = 16
TOKENS = 192
VOCAB = 143360
OWNERS = 32
N_ROWS = 32


def head_matrix(key, width, salt):
    key = jax.random.fold_in(key, salt)
    noise = jnp.clip(jax.random.normal(key, (width, VOCAB), jnp.float32), -3.3, 3.3)
    return noise * (3.0 / width ** 0.5)


def broad_rows(key, width):
    position = jnp.arange(TOKENS)
    noise = jnp.clip(jax.random.normal(key, (TOKENS, width), jnp.float32), -4.0, 4.0)
    wide = jnp.clip(6.0 * jax.random.normal(jax.random.fold_in(key, 5), (TOKENS, width), jnp.float32), -12.0, 12.0)
    return jnp.where((position % 8 == 4)[:, None], wide, noise)


def draw_student_head(key, part):
    return head_matrix(key, DS, 101).astype(jnp.bfloat16)


def draw_teacher_head(key, part):
    return head_matrix(key, DT, 202).astype(jnp.bfloat16)


def draw_student_hidden(key, part):
    key = jax.random.fold_in(key, 11)
    return broad_rows(key, DS).astype(jnp.bfloat16)


def draw_teacher_hidden(key, part):
    key = jax.random.fold_in(key, 13)
    return broad_rows(key, DT).astype(jnp.bfloat16)


def set_ends(drawn, rng, low, largest):
    shape = drawn.shape
    place = [jax.random.randint(jax.random.fold_in(rng, axis), (), 0, shape[axis]) for axis in range(len(shape))]
    drawn = drawn.at[tuple(place)].set(low)
    longest = shape.index(max(shape))
    place[longest] = (place[longest] + 1) % shape[longest]
    return drawn.at[tuple(place)].set(largest)


def length_profile(number_of, total, reach, skew):
    weights = [(1 << 20) // math.isqrt(grade ** skew) + 1 for grade in range(2, number_of + 1)]
    rest, given = total - reach - (number_of - 1), [1] * (number_of - 1)
    while rest > 0:
        candidates = [i for i in range(number_of - 1) if given[i] < reach]
        mass, remaining = sum([weights[i] for i in candidates]), rest
        for i in candidates:
            extra = min(reach - given[i], max(1, remaining * weights[i] // mass), rest)
            given[i] = given[i] + extra
            rest = rest - extra
    return np.array([reach] + given)


def uneven_parts(own_key, amount, total, most, lean):
    if amount == 2:
        one = jax.random.randint(own_key, (), max(1, total - most), min(most, total - 1) + 1)
        return jnp.stack([one, total - one])
    lengths = jnp.asarray(length_profile(amount, total, most, lean), jnp.int32)
    twos = (amount - 1) // 2
    giver, taker = lengths[1:1 + 2 * twos:2], lengths[2:2 + 2 * twos:2]
    margin = jnp.minimum(giver - 1, most - taker)
    shifted = jax.random.randint(jax.random.fold_in(own_key, 1), (twos,), 0, 1 << 20) % (margin + 1)
    lengths = lengths.at[1:1 + 2 * twos:2].set(giver - shifted).at[2:2 + 2 * twos:2].set(taker + shifted)
    return lengths[jax.random.permutation(jax.random.fold_in(own_key, 2), amount)]


def setup_inputs(seed: int = 0) -> dict:
    splits = jax.random.split(jax.random.key(seed), 9)
    student_hidden = draw_student_hidden(jax.random.fold_in(splits[8], 71), 0)
    teacher_hidden = draw_teacher_hidden(jax.random.fold_in(splits[8], 71), 0)
    student_head = draw_student_head(jax.random.fold_in(splits[8], 71), 0)
    teacher_head = draw_teacher_head(jax.random.fold_in(splits[8], 71), 0)
    teacher_row = jax.random.permutation(splits[4], TOKENS).astype(jnp.int32)
    live_counts = uneven_parts(splits[5], OWNERS, N_ROWS * (TOK_DEV + 1) // 2, TOK_DEV, 2).astype(jnp.int32)
    branch_id = set_ends(jax.random.randint(splits[6], (TOKENS,), 0, NBR), jax.random.fold_in(splits[6], 1), 0, NBR - 1).astype(jnp.int32)
    branch_ratio = jnp.clip(jnp.exp(jax.random.uniform(splits[7], (NBR,), jnp.float32, math.log(0.25), math.log(4.0))), 0.25, 4.0)
    return dict(student_hidden=student_hidden, teacher_hidden=teacher_hidden, student_head=student_head, teacher_head=teacher_head, teacher_row=teacher_row, live_counts=live_counts, branch_id=branch_id, branch_ratio=branch_ratio)


def reference(student_hidden, teacher_hidden, student_head, teacher_head, teacher_row, live_counts, branch_id, branch_ratio):
    student_logits = jnp.dot(student_hidden, student_head, preferred_element_type=jnp.float32)
    teacher_ordered = jnp.take(teacher_hidden, teacher_row, axis=0)
    teacher_logits = jnp.dot(teacher_ordered, teacher_head, preferred_element_type=jnp.float32)
    student_logp = student_logits - jax.nn.logsumexp(student_logits, axis=1, keepdims=True)
    teacher_logp = teacher_logits - jax.nn.logsumexp(teacher_logits, axis=1, keepdims=True)
    student_prob = jnp.exp(student_logp)
    log_gap = student_logp - teacher_logp
    divergence = jnp.sum(student_prob * log_gap, axis=1)
    position = jnp.arange(TOKENS, dtype=jnp.int32)
    owner_live = jnp.take(live_counts, position // TOK_DEV, axis=0)
    live = ((position % TOK_DEV) < owner_live).astype(jnp.float32)
    weight = live * jnp.take(branch_ratio, branch_id, axis=0)
    token_loss = weight * divergence
    logit_grad = (weight[:, None] * student_prob * (log_gap - divergence[:, None])).astype(jnp.bfloat16)
    grad_hidden = jnp.dot(logit_grad, student_head.T, preferred_element_type=jnp.float32)
    return token_loss, grad_hidden
```

```python
import functools

import jax
import jax.numpy as jnp
from jax import lax
from jax.experimental import pallas as pl
from jax.experimental.pallas import tpu as pltpu
from jax.sharding import PartitionSpec as P

MESH = pl.DeviceIdType.MESH
F32 = jnp.float32
BF16 = jnp.bfloat16
LIVE = 112
HALF = 288

SIB_P, SIB_X, SIB_ST, SIB_R1, SIB_R5 = 0, 1, 17, 18, 22
ZF, ZN, ZST, ZR = 23, 26, 29, 44
PA, PB, PST, R2, R3 = 59, 62, 74, 89, 92
N_SEMS = 95


def iota(shape, dim):
    return lax.broadcasted_iota(jnp.int32, shape, dim)


def sixth(n):
    return lax.shift_right_logical(n * 171, 10)


def as_col(row, n):
    eye = iota((n, n), 0) == iota((n, n), 1)
    return jnp.sum(jnp.where(eye, row, 0.0), axis=1, keepdims=True)


def as_row(col, n):
    eye = iota((n, n), 0) == iota((n, n), 1)
    return jnp.sum(jnp.where(eye, col, 0.0), axis=0, keepdims=True)


def merge(stats):
    part = [stats[:, k, :] for k in range(5)]
    peak_s = jnp.max(part[0], axis=0, keepdims=True)
    peak_t = jnp.max(part[1], axis=0, keepdims=True)
    scale_s = jnp.exp(part[0] - peak_s)
    scale_t = jnp.exp(part[1] - peak_t)
    sum_s = jnp.sum(scale_s * part[2], axis=0, keepdims=True)
    sum_t = jnp.sum(scale_t * part[3], axis=0, keepdims=True)
    cross = jnp.sum(scale_s * part[4], axis=0, keepdims=True)
    return peak_s, peak_t, sum_s, sum_t, cross


def put_stats(ref, parts):
    row = iota((8, 128), 0)
    out = jnp.zeros((8, 128), F32)
    for k, part in enumerate(parts):
        out = jnp.where(row == k, part, out)
    ref[...] = out


def kernel(
    stop,
    sh_ref, th_ref, ws_hbm, wt_hbm, trow_ref, live_ref, branch_ref, ratio_ref,
    loss_ref, grad_ref,
    ws, wt, wide, parts, zbuf, sel, xbuf, logits, un1, un2, st_a, st_b, st_c,
    gt, sib_out, rb1, sb2, rb2, acc2, sb3, rb3, place, sb4, rb4, sb5, rb5, tail,
    head_sem, send, recv,
):
    r = lax.axis_index("rows")
    v = lax.axis_index("vocab")
    z = lax.div(r, 2)
    c = lax.rem(r, 2)
    x = lax.div(v, 4)
    y = lax.rem(v, 4)
    o = 1 - c
    a = x * o + y * c
    b = y * o + x * c

    def v_of(pa, pb):
        return (pa * 4 + pb) * o + (pb * 4 + pa) * c

    def v_sib(pa, pb):
        return (pa * 4 + pb) * c + (pb * 4 + pa) * o

    sibling = (z * 2 + o, v)

    def z_dev(d):
        return (lax.rem(z + d, 16) * 2 + c, v)

    def plane_dev(da, db):
        return (r, v_of(lax.rem(a + da, 4), lax.rem(b + db, 4)))

    def rcopy(src, dst, number, device):
        return pltpu.make_async_remote_copy(
            src_ref=src, dst_ref=dst, send_sem=send.at[number], recv_sem=recv.at[number],
            device_id=device, device_id_type=MESH,
        )

    pending = []

    def go(src, dst, number, device):
        copy = rcopy(src, dst, number, device)
        copy.start()
        pending.append(copy)

    def arrive(dst, number):
        rcopy(dst, dst, number, sibling).wait_recv()

    heads = [
        pltpu.make_async_copy(ws_hbm, ws, head_sem.at[0]),
        pltpu.make_async_copy(wt_hbm, wt, head_sem.at[1]),
    ]
    for copy in heads:
        copy.start()

    plane = [(da, db) for da in range(4) for db in range(4) if (da, db) != (0, 0)]
    barrier = pltpu.get_barrier_semaphore()
    pl.semaphore_signal(barrier, inc=1, device_id=sibling, device_id_type=MESH)
    for d in range(1, 16):
        pl.semaphore_signal(barrier, inc=1, device_id=z_dev(d), device_id_type=MESH)
    for da, db in plane:
        pl.semaphore_signal(barrier, inc=1, device_id=plane_dev(da, db), device_id_type=MESH)

    row16 = iota((16, 128), 0)
    wide[...] = jnp.zeros_like(wide)
    wide[0:6, 0:320] = sh_ref[...].astype(F32)
    sw = wide[...]
    s2 = sw[:, 256:384]
    s2_high = pltpu.roll(s2, 64, 1)
    th = th_ref[...].astype(F32)
    pack_s = jnp.zeros((16, 128), F32)
    pack_t = jnp.zeros((16, 128), F32)
    for i in range(6):
        pack_s = jnp.where(row16 == i, sw[i:i + 1, 0:128], pack_s)
        pack_s = jnp.where(row16 == 6 + i, sw[i:i + 1, 128:256], pack_s)
        pack_t = jnp.where(row16 == i, th[i:i + 1, 0:128], pack_t)
        pack_t = jnp.where(row16 == 6 + i, th[i:i + 1, 128:256], pack_t)
    for i in range(3):
        pack_s = jnp.where(row16 == 12 + i, s2[i:i + 1, :] + s2_high[i + 3:i + 4, :], pack_s)
    parts[0] = pack_s.astype(BF16)
    parts[1] = pack_t.astype(BF16)
    z_group = lax.rem(z, 4)
    z_slot = z_group * 4 + lax.div(z, 4)
    zbuf[z_slot, c] = parts[c]

    pl.semaphore_wait(barrier, 31)

    go(parts.at[o], zbuf.at[z_slot, c], SIB_P, sibling)

    live_row = live_ref[...].astype(F32)
    live_col = as_col(live_row, 32)
    owner_a, owner_b = iota((32, 32), 0), iota((32, 32), 1)
    before_col = jnp.sum(jnp.where(owner_b < owner_a, live_row, 0.0), axis=1, keepdims=True)
    before_row = jnp.sum(jnp.where(owner_a < owner_b, live_col, 0.0), axis=0, keepdims=True)
    pos = iota((1, 192), 1)
    pos_owner = sixth(pos)
    pos_slot = (pos - 6 * pos_owner).astype(F32)
    own = iota((32, 192), 0) == sixth(iota((32, 192), 1))
    rank = jnp.sum(jnp.where(own, before_col, 0.0), axis=0, keepdims=True) + pos_slot
    alive = jnp.sum(jnp.where(own, live_col, 0.0), axis=0, keepdims=True) > pos_slot
    rank = jnp.where(alive, rank, -1.0).astype(jnp.int32)
    pick = iota((128, 192), 0) == rank
    pos_of = jnp.sum(jnp.where(pick, pos.astype(F32), 0.0), axis=1, keepdims=True)
    teacher_of = jnp.sum(jnp.where(pick, trow_ref[...].astype(F32), 0.0), axis=1, keepdims=True)
    ratio_col = as_col(ratio_ref[...], 16)
    ratio_of = jnp.sum(
        jnp.where(iota((16, 192), 0) == branch_ref[...], ratio_col, 0.0), axis=0, keepdims=True
    )
    weight = as_row(jnp.sum(jnp.where(pick, ratio_of, 0.0), axis=1, keepdims=True), 128)
    source = jnp.where(c == 0, pos_of, teacher_of).astype(jnp.int32)[0:LIVE]
    src_owner = sixth(source)
    src_slot = source - 6 * src_owner
    src_z = lax.shift_right_logical(src_owner, 1)
    base = (
        (jnp.bitwise_and(src_z, 3) * 4 + lax.shift_right_logical(src_z, 2)) * 32
        + jnp.bitwise_and(src_owner, 1) * 16
    )
    low = src_slot < 3
    column = iota((LIVE, 512), 1)
    for k, at in enumerate((
        base + src_slot, base + 6 + src_slot, base + 12 + jnp.where(low, src_slot, src_slot - 3)
    )):
        sel[k] = jnp.where(column == at, 1.0, 0.0).astype(BF16)

    arrive(zbuf.at[z_slot, o], SIB_P)
    for n, d in enumerate((8, 4, 12)):
        go(zbuf.at[z_slot], zbuf.at[z_slot], ZF + n, z_dev(d))

    dest = iota((256, 1), 0)
    dest_z, q = lax.shift_right_logical(dest, 4), jnp.bitwise_and(dest, 15)

    def back(row, wanted):
        second = jnp.where(row >= 6, 1, 0)
        owner = 2 * dest_z + second
        slot = (row - 6 * second).astype(F32)
        mine = iota((256, 32), 1) == owner
        start = jnp.sum(jnp.where(mine, before_row, 0.0), axis=1, keepdims=True)
        count = jnp.sum(jnp.where(mine, live_row, 0.0), axis=1, keepdims=True)
        j = jnp.where(wanted & (slot < count), start + slot, -1.0).astype(jnp.int32)
        return jnp.where(iota((256, 128), 1) == j, 1.0, 0.0).astype(BF16)

    un1[...] = back(q, q < 12)
    for g in range(4):
        un2[g] = back((q - 12) * 4 + g, (q >= 12) & (q < 15))

    for n, d in enumerate((8, 4, 12)):
        arrive(zbuf.at[z_group * 4 + lax.rem(lax.div(z, 4) + 4 - d // 4, 4)], ZF + n)
    group = zbuf.at[pl.ds(z_group * 4, 4)]
    for n, d in enumerate((1, 15, 2)):
        go(group, group, ZN + n, z_dev(d))
    for n, d in enumerate((1, 15, 2)):
        arrive(zbuf.at[pl.ds(lax.rem(z_group + 16 - d, 4) * 4, 4)], ZN + n)

    if stop >= 2:
        raw = zbuf[...].reshape(512, 128)
        chunk = [jnp.dot(sel[k], raw, preferred_element_type=F32) for k in range(3)]
        turned = pltpu.roll(chunk[2], 64, 1)
        lane = iota((64, 128), 1)
        packed = jnp.where(
            lane < 64,
            jnp.where(low, chunk[2], turned)[0:64],
            jnp.where(low, turned, chunk[2])[48:112],
        )
        xbuf[c, v, 0:112] = chunk[0].astype(BF16)
        xbuf[c, v, 112:224] = chunk[1].astype(BF16)
        xbuf[c, v, 224:288] = packed.astype(BF16)

        def spread(pa, n):
            block = xbuf.at[c, v_of(pa, b)]
            for k, d in enumerate((2, 1, 3)):
                go(block, block, PB + 3 * n + k, plane_dev(0, d))
            go(block, block, SIB_X + n, sibling)

        mine = xbuf.at[c, v]
        for k, d in enumerate((1, 3, 2)):
            go(mine, mine, PA + k, plane_dev(d, 0))
        spread(a, 0)
        for k, d in enumerate((1, 3, 2)):
            pa = lax.rem(a + 4 - d, 4)
            arrive(xbuf.at[c, v_of(pa, b)], PA + k)
            spread(pa, k + 1)
        for n, d0 in enumerate((0, 1, 3, 2)):
            for k, d in enumerate((2, 1, 3)):
                block = xbuf.at[c, v_of(lax.rem(a + 4 - d0, 4), lax.rem(b + 4 - d, 4))]
                arrive(block, PB + 3 * n + k)
                go(block, block, SIB_X + 4 + 3 * n + k, sibling)
        for n, d0 in enumerate((0, 1, 3, 2)):
            pa = lax.rem(b + 4 - d0, 4)
            arrive(xbuf.at[o, v_sib(pa, a)], SIB_X + n)
        for n, d0 in enumerate((0, 1, 3, 2)):
            for k, d in enumerate((2, 1, 3)):
                pa, pb = lax.rem(b + 4 - d0, 4), lax.rem(a + 4 - d, 4)
                arrive(xbuf.at[o, v_sib(pa, pb)], SIB_X + 4 + 3 * n + k)
    for copy in heads:
        copy.wait()

    if stop >= 3:
        lane = iota((LIVE, 128), 1)
        keep = (lane < 64) == (iota((LIVE, 128), 0) < 64)
        acc_s = jnp.zeros((LIVE, 280), F32)
        acc_t = jnp.zeros((LIVE, 280), F32)
        for pair in range(8):
            left, right = [], []
            for w in (2 * pair, 2 * pair + 1):
                block = jnp.concatenate([xbuf[0, w, 0:112], xbuf[0, w, 112:224]], axis=1)
                acc_s += jnp.dot(block, ws[w * 320:w * 320 + 256], preferred_element_type=F32)
                block = jnp.concatenate([xbuf[1, w, 0:112], xbuf[1, w, 112:224]], axis=1)
                acc_t += jnp.dot(block, wt[w * 256:w * 256 + 256], preferred_element_type=F32)
                rest = jnp.concatenate([xbuf[0, w, 224:288], xbuf[0, w, 240:288]], axis=0)
                left.append(jnp.where(keep, rest, jnp.zeros_like(rest)))
                right += [ws[w * 320 + 256:w * 320 + 320]] * 2
            acc_s += jnp.dot(
                jnp.concatenate(left, axis=1), jnp.concatenate(right, axis=0),
                preferred_element_type=F32,
            )
        logits[...] = jnp.zeros_like(logits)
        logits[0, 0:LIVE, 0:280] = acc_s
        logits[1, 0:LIVE, 0:280] = acc_t
        student = jnp.transpose(logits[0])[0:280]
        teacher = jnp.transpose(logits[1])[0:280]
        diff = student - teacher
        peak_s = jnp.max(student, axis=0, keepdims=True)
        peak_t = jnp.max(teacher, axis=0, keepdims=True)
        expo = jnp.exp(student - peak_s)
        put_stats(st_a.at[c], (
            peak_s, peak_t,
            jnp.sum(expo, axis=0, keepdims=True),
            jnp.sum(jnp.exp(teacher - peak_t), axis=0, keepdims=True),
            jnp.sum(expo * diff, axis=0, keepdims=True),
        ))

    if stop >= 4:
        go(st_a.at[c], st_a.at[c], SIB_ST, sibling)
        arrive(st_a.at[o], SIB_ST)
        put_stats(st_b.at[v], merge(st_a[...]))
        for n, (da, db) in enumerate(plane):
            go(st_b.at[v], st_b.at[v], PST + n, plane_dev(da, db))
        for n, (da, db) in enumerate(plane):
            arrive(st_b.at[v_of(lax.rem(a + 4 - da, 4), lax.rem(b + 4 - db, 4))], PST + n)
        put_stats(st_c.at[z], merge(st_b[...]))
        for n, d in enumerate(range(1, 16)):
            go(st_c.at[z], st_c.at[z], ZST + n, z_dev(d))
        for n, d in enumerate(range(1, 16)):
            arrive(st_c.at[lax.rem(z + 16 - d, 16)], ZST + n)
        peak_s, peak_t, sum_s, sum_t, cross = merge(st_c[...])
        lse_s = peak_s + jnp.log(sum_s)
        lse_t = peak_t + jnp.log(sum_t)
        divergence = cross / sum_s - lse_s + lse_t
        loss = as_col(weight * divergence, 128)
        ours = iota((1, 32), 1) == r
        start = jnp.sum(jnp.where(ours, before_row, 0.0), axis=1, keepdims=True)
        count = jnp.sum(jnp.where(ours, live_row, 0.0), axis=1, keepdims=True)
        slot = iota((1, 128), 1).astype(F32)
        at = jnp.where(slot < count, start + slot, -1.0).astype(jnp.int32)
        loss_ref[...] = jnp.sum(
            jnp.where(iota((128, 128), 0) == at, loss, 0.0), axis=0, keepdims=True
        )
        gt[...] = (
            weight * jnp.exp(student - lse_s) * (diff - lse_s + lse_t - divergence)
        ).astype(BF16)

    if stop >= 5:
        order = (2, 1, 3, 0)
        g = gt[...]

        def back_product(w, half):
            at = pl.multiple_of(w * 320 + half * 160, 32)
            return jnp.dot(ws[pl.ds(at, 160), :], g, preferred_element_type=F32)

        for d in order:
            pb = lax.rem(a + d, 4)
            for pa in range(4):
                sib_out[d, pa] = back_product(v_sib(pa, pb), o).astype(BF16)
            go(sib_out.at[d], rb1.at[d], SIB_R1 + d, sibling)
        for d in order:
            pb = lax.rem(b + d, 4)
            arrive(rb1.at[d], SIB_R1 + d)
            for pa in range(4):
                total = back_product(v_of(pa, pb), c) + rb1[d, pa].astype(F32)
                if d:
                    sb2[d - 1, pa] = total.astype(BF16)
                else:
                    acc2[pa] = total
            if d:
                go(sb2.at[d - 1], rb2.at[d - 1], R2 + d - 1, plane_dev(0, d))
        for d in (1, 3, 2):
            arrive(rb2.at[d - 1], R2 + d - 1)
        for d in (2, 1, 3, 0):
            pa = lax.rem(a + d, 4)
            total = acc2[pa]
            for k in range(3):
                total += rb2[k, pa].astype(F32)
            if d:
                sb3[d - 1] = total.astype(BF16)
                go(sb3.at[d - 1], rb3.at[d - 1], R3 + d - 1, plane_dev(d, 0))
        for d in (1, 3, 2):
            arrive(rb3.at[d - 1], R3 + d - 1)
            total += rb3[d - 1].astype(F32)
        total = total.astype(BF16)

    if stop >= 6:
        place[...] = jnp.zeros_like(place)
        for k in range(4):
            place[k, 32 * k:32 * k + 32] = total[128:160]
        nt = (((1,), (1,)), ((), ()))
        spread_out = lax.dot_general(un1[...], total[0:128], nt, preferred_element_type=F32)
        for k in range(4):
            spread_out += lax.dot_general(un2[k], place[k], nt, preferred_element_type=F32)
        sb4[...] = spread_out.astype(BF16).reshape(16, 16, 128)
        rb4[z] = sb4[z]
        for n, d in enumerate(range(1, 16)):
            go(sb4.at[lax.rem(z + d, 16)], rb4.at[z], ZR + n, z_dev(d))
        for n, d in enumerate(range(1, 16)):
            arrive(rb4.at[lax.rem(z + 16 - d, 16)], ZR + n)
        full = jnp.sum(rb4[...].astype(F32), axis=0)
        sb5[c] = full
        go(sb5.at[c], sb5.at[c], SIB_R5, sibling)
        arrive(sb5.at[o], SIB_R5)
        grads = []
        for h in range(2):
            block = sb5[h]
            for row in range(12):
                at = 32 * (row % 4)
                tail[h, row:row + 1, 0:32] = block[12 + row // 4:13 + row // 4, at:at + 32]
            grads.append(jnp.where(c == 0, block[0:6], block[6:12]))
            grads.append(jnp.where(c == 0, tail[h, 0:6], tail[h, 6:12])[:, 0:32])
        grad_ref[:, 0:128] = grads[0]
        grad_ref[:, 128:160] = grads[1]
        grad_ref[:, 160:288] = grads[2]
        grad_ref[:, 288:320] = grads[3]
    else:
        grad_ref[...] = jnp.zeros_like(grad_ref)
        if stop < 4:
            loss_ref[...] = jnp.zeros_like(loss_ref)

    for copy in pending:
        copy.wait_send()


def on_device(
    student_hidden, teacher_hidden, student_head, teacher_head,
    teacher_row, live_counts, branch_id, branch_ratio, stop=99,
):
    vmem = pl.BlockSpec(memory_space=pltpu.VMEM)
    hbm = pl.BlockSpec(memory_space=pl.ANY)
    loss, grad = pl.pallas_call(
        functools.partial(kernel, stop),
        out_shape=(
            jax.ShapeDtypeStruct((1, 128), F32),
            jax.ShapeDtypeStruct((6, 320), F32),
        ),
        in_specs=[vmem, vmem, hbm, hbm, vmem, vmem, vmem, vmem],
        out_specs=(vmem, vmem),
        scratch_shapes=[
            pltpu.VMEM((5120, 280), BF16),
            pltpu.VMEM((4096, 280), BF16),
            pltpu.VMEM((8, 384), F32),
            pltpu.VMEM((2, 16, 128), BF16),
            pltpu.VMEM((16, 2, 16, 128), BF16),
            pltpu.VMEM((3, LIVE, 512), BF16),
            pltpu.VMEM((2, 16, HALF, 128), BF16),
            pltpu.VMEM((2, 128, 384), F32),
            pltpu.VMEM((256, 128), BF16),
            pltpu.VMEM((4, 256, 128), BF16),
            pltpu.VMEM((2, 8, 128), F32),
            pltpu.VMEM((16, 8, 128), F32),
            pltpu.VMEM((16, 8, 128), F32),
            pltpu.VMEM((280, 128), BF16),
            pltpu.VMEM((4, 4, 160, 128), BF16),
            pltpu.VMEM((4, 4, 160, 128), BF16),
            pltpu.VMEM((3, 4, 160, 128), BF16),
            pltpu.VMEM((3, 4, 160, 128), BF16),
            pltpu.VMEM((4, 160, 128), F32),
            pltpu.VMEM((3, 160, 128), BF16),
            pltpu.VMEM((3, 160, 128), BF16),
            pltpu.VMEM((4, 128, 128), BF16),
            pltpu.VMEM((16, 16, 128), BF16),
            pltpu.VMEM((16, 16, 128), BF16),
            pltpu.VMEM((2, 16, 128), F32),
            pltpu.VMEM((8, 128), F32),
            pltpu.VMEM((2, 16, 128), F32),
            pltpu.SemaphoreType.DMA((2,)),
            pltpu.SemaphoreType.DMA((N_SEMS,)),
            pltpu.SemaphoreType.DMA((N_SEMS,)),
        ],
        compiler_params=pltpu.CompilerParams(
            collective_id=0, has_side_effects=True, vmem_limit_bytes=48 * 1024 * 1024
        ),
    )(
        student_hidden, teacher_hidden, student_head, teacher_head,
        teacher_row.reshape(1, -1), live_counts.reshape(1, -1),
        branch_id.reshape(1, -1), branch_ratio.reshape(1, -1),
    )
    return loss[0, 0:6], grad


def solution(mesh, stop=99):
    in_specs = (
        P("rows", "vocab"),
        P("rows", "vocab"),
        P(None, ("rows", "vocab")),
        P(None, ("rows", "vocab")),
        P(),
        P(),
        P(),
        P(),
    )
    out_specs = (P("rows"), P("rows", "vocab"))
    return jax.shard_map(
        functools.partial(on_device, stop=stop), mesh=mesh, in_specs=in_specs,
        out_specs=out_specs, check_vma=False,
    )
```

```python
import jax
import jax.numpy as jnp
from jax import lax
from jax.experimental import pallas as pl
from jax.experimental.pallas import tpu as pltpu
from jax.sharding import PartitionSpec as P

MESH = pl.DeviceIdType.MESH
F32 = jnp.float32
BF16 = jnp.bfloat16
LIVE = 112
HALF = 288

SIB_P, SIB_X, SIB_ST, SIB_W, SIB_G, SIB_R5 = 0, 1, 17, 18, 20, 21
ZP, ZST, ZR = 22, 37, 52
PA, PB, PST, R2, R3 = 67, 70, 82, 97, 100
N_SEMS = 103
Z_ORDER = (8, 7, 9, 6, 10, 5, 11, 4, 12, 3, 13, 2, 14, 1, 15)


def iota(shape, dim):
    return lax.broadcasted_iota(jnp.int32, shape, dim)


def sixth(n):
    return lax.shift_right_logical(n * 171, 10)


def as_col(row, n):
    eye = iota((n, n), 0) == iota((n, n), 1)
    return jnp.sum(jnp.where(eye, row, 0.0), axis=1, keepdims=True)


def as_row(col, n):
    eye = iota((n, n), 0) == iota((n, n), 1)
    return jnp.sum(jnp.where(eye, col, 0.0), axis=0, keepdims=True)


def merge(stats):
    part = [stats[:, k, :] for k in range(5)]
    peak_s = jnp.max(part[0], axis=0, keepdims=True)
    peak_t = jnp.max(part[1], axis=0, keepdims=True)
    scale_s = jnp.exp(part[0] - peak_s)
    scale_t = jnp.exp(part[1] - peak_t)
    sum_s = jnp.sum(scale_s * part[2], axis=0, keepdims=True)
    sum_t = jnp.sum(scale_t * part[3], axis=0, keepdims=True)
    cross = jnp.sum(scale_s * part[4], axis=0, keepdims=True)
    return peak_s, peak_t, sum_s, sum_t, cross


def put_stats(ref, parts):
    row = iota((8, 128), 0)
    out = jnp.zeros((8, 128), F32)
    for k, part in enumerate(parts):
        out = jnp.where(row == k, part, out)
    ref[...] = out


def kernel(
    sh_hbm, th_hbm, ws_hbm, wt_hbm, trow_hbm, live_hbm, branch_hbm, ratio_hbm,
    loss_ref, grad_ref,
    sh_ref, th_ref, trow_ref, live_ref, branch_ref, ratio_ref,
    wst, wtt, wh, wsib, wide, parts, zbuf, sel, xbuf, un1, un2, st_a, st_b, st_c,
    g2, sb2, rb2, acc2, sb3, rb3, place, sb4, rb4, sb5, tail,
    head_sem, small_sem, send, recv,
):
    r = lax.axis_index("rows")
    v = lax.axis_index("vocab")
    z = lax.div(r, 2)
    c = lax.rem(r, 2)
    x = lax.div(v, 4)
    y = lax.rem(v, 4)
    o = 1 - c
    a = x * o + y * c
    b = y * o + x * c

    def v_of(pa, pb):
        return (pa * 4 + pb) * o + (pb * 4 + pa) * c

    def v_sib(pa, pb):
        return (pa * 4 + pb) * c + (pb * 4 + pa) * o

    sibling = (z * 2 + o, v)

    def z_dev(d):
        return (lax.rem(z + d, 16) * 2 + c, v)

    def plane_dev(da, db):
        return (r, v_of(lax.rem(a + da, 4), lax.rem(b + db, 4)))

    def rcopy(src, dst, number, device):
        return pltpu.make_async_remote_copy(
            src_ref=src, dst_ref=dst, send_sem=send.at[number], recv_sem=recv.at[number],
            device_id=device, device_id_type=MESH,
        )

    pending = []

    def go(src, dst, number, device):
        copy = rcopy(src, dst, number, device)
        copy.start()
        pending.append(copy)

    def arrive(dst, number):
        rcopy(dst, dst, number, sibling).wait_recv()

    heads = [
        pltpu.make_async_copy(ws_hbm, wst, head_sem.at[0]),
        pltpu.make_async_copy(wt_hbm, wtt, head_sem.at[1]),
    ]
    small = [
        pltpu.make_async_copy(src, dst, small_sem.at[n])
        for n, (src, dst) in enumerate((
            (sh_hbm, sh_ref), (th_hbm, th_ref), (trow_hbm, trow_ref),
            (live_hbm, live_ref), (branch_hbm, branch_ref), (ratio_hbm, ratio_ref),
        ))
    ]
    for copy in small + heads:
        copy.start()

    plane = [(da, db) for da in range(4) for db in range(4) if (da, db) != (0, 0)]
    plane.sort(key=lambda at: -min(at[0], 4 - at[0]) - min(at[1], 4 - at[1]))
    barrier = pltpu.get_barrier_semaphore()
    for d in Z_ORDER:
        pl.semaphore_signal(barrier, inc=1, device_id=z_dev(d), device_id_type=MESH)
    for da, db in plane:
        pl.semaphore_signal(barrier, inc=1, device_id=plane_dev(da, db), device_id_type=MESH)
    pl.semaphore_signal(barrier, inc=1, device_id=sibling, device_id_type=MESH)
    for copy in small:
        copy.wait()

    row16 = iota((16, 128), 0)
    wide[...] = jnp.zeros_like(wide)
    wide[0:6, 0:320] = sh_ref[...].astype(F32)
    sw = wide[...]
    odd = lax.rem(v, 2) == 1
    sw_odd = jnp.concatenate([pltpu.roll(sw, 320, 1)[:, 0:256], sw[:, 0:128]], axis=1)
    sw = jnp.where(odd, sw_odd, sw)
    s2 = jnp.where(iota((8, 128), 1) < 64, sw[:, 256:384], 0.0)
    s2_high = pltpu.roll(s2, 64, 1)
    th = th_ref[...].astype(F32)
    pack_s = jnp.zeros((16, 128), F32)
    pack_t = jnp.zeros((16, 128), F32)
    for i in range(6):
        pack_s = jnp.where(row16 == i, sw[i:i + 1, 0:128], pack_s)
        pack_s = jnp.where(row16 == 6 + i, sw[i:i + 1, 128:256], pack_s)
        pack_t = jnp.where(row16 == i, th[i:i + 1, 0:128], pack_t)
        pack_t = jnp.where(row16 == 6 + i, th[i:i + 1, 128:256], pack_t)
    for i in range(3):
        pack_s = jnp.where(row16 == 12 + i, s2[i:i + 1, :] + s2_high[i + 3:i + 4, :], pack_s)
    parts[0] = pack_s.astype(BF16)
    parts[1] = pack_t.astype(BF16)
    zbuf[z, c] = parts[c]

    live_row = live_ref[...].astype(F32)
    live_col = as_col(live_row, 32)
    owner_a, owner_b = iota((32, 32), 0), iota((32, 32), 1)
    before_col = jnp.sum(jnp.where(owner_b < owner_a, live_row, 0.0), axis=1, keepdims=True)
    before_row = jnp.sum(jnp.where(owner_a < owner_b, live_col, 0.0), axis=0, keepdims=True)
    pos = iota((1, 192), 1)
    pos_owner = sixth(pos)
    pos_slot = (pos - 6 * pos_owner).astype(F32)
    own = iota((32, 192), 0) == sixth(iota((32, 192), 1))
    rank = jnp.sum(jnp.where(own, before_col, 0.0), axis=0, keepdims=True) + pos_slot
    alive = jnp.sum(jnp.where(own, live_col, 0.0), axis=0, keepdims=True) > pos_slot
    rank = jnp.where(alive, rank, -1.0).astype(jnp.int32)
    pick = iota((128, 192), 0) == rank
    pos_of = jnp.sum(jnp.where(pick, pos.astype(F32), 0.0), axis=1, keepdims=True)
    teacher_of = jnp.sum(jnp.where(pick, trow_ref[...].astype(F32), 0.0), axis=1, keepdims=True)
    ratio_col = as_col(ratio_ref[...], 16)
    ratio_of = jnp.sum(
        jnp.where(iota((16, 192), 0) == branch_ref[...], ratio_col, 0.0), axis=0, keepdims=True
    )
    weight = as_row(jnp.sum(jnp.where(pick, ratio_of, 0.0), axis=1, keepdims=True), 128)
    source = jnp.where(c == 0, pos_of, teacher_of).astype(jnp.int32)[0:LIVE]
    src_owner = sixth(source)
    src_slot = source - 6 * src_owner
    src_z = lax.shift_right_logical(src_owner, 1)
    base = src_z * 32 + jnp.bitwise_and(src_owner, 1) * 16
    low = src_slot < 3
    column = iota((LIVE, 512), 1)
    for k, at in enumerate((
        base + src_slot, base + 6 + src_slot, base + 12 + jnp.where(low, src_slot, src_slot - 3)
    )):
        sel[k] = jnp.where(column == at, 1.0, 0.0).astype(BF16)

    dest = iota((256, 1), 0)
    dest_z, q = lax.shift_right_logical(dest, 4), jnp.bitwise_and(dest, 15)

    def back(row, wanted):
        second = jnp.where(row >= 6, 1, 0)
        owner = 2 * dest_z + second
        slot = (row - 6 * second).astype(F32)
        mine = iota((256, 32), 1) == owner
        start = jnp.sum(jnp.where(mine, before_row, 0.0), axis=1, keepdims=True)
        count = jnp.sum(jnp.where(mine, live_row, 0.0), axis=1, keepdims=True)
        j = jnp.where(wanted & (slot < count), start + slot, -1.0).astype(jnp.int32)
        return jnp.where(iota((256, 128), 1) == j, 1.0, 0.0).astype(BF16)

    un1[...] = back(q, q < 12)
    for g in range(4):
        un2[g] = back((q - 12) * 4 + g, (q >= 12) & (q < 15))

    pl.semaphore_wait(barrier, 31)
    go(parts.at[o], zbuf.at[z, c], SIB_P, sibling)
    arrive(zbuf.at[z, o], SIB_P)
    for n, d in enumerate(Z_ORDER):
        go(zbuf.at[z], zbuf.at[z], ZP + n, z_dev(d))

    heads[0].wait()
    for part in range(2):
        for u in range(4 * part, 4 * part + 4):
            turned = jnp.transpose(wst[:, 640 * u:640 * u + 640])
            for k in range(4):
                wh[k % 2, 2 * u + k // 2] = turned[160 * k:160 * k + 160]
        where = pl.ds(8 * part, 8)
        go(wh.at[o, where], wsib.at[where], SIB_W + part, sibling)
    for n, d in enumerate(Z_ORDER):
        arrive(zbuf.at[lax.rem(z + 16 - d, 16)], ZP + n)
    for part in range(2):
        where = pl.ds(8 * part, 8)
        arrive(wsib.at[where], SIB_W + part)
    raw = zbuf[...].reshape(512, 128)
    chunk = [jnp.dot(sel[k], raw, preferred_element_type=F32) for k in range(3)]
    turned = pltpu.roll(chunk[2], 64, 1)
    lane = iota((64, 128), 1)
    in_low, in_high = jnp.where(low, chunk[2], turned), jnp.where(low, turned, chunk[2])
    packed = jnp.where(
        odd,
        jnp.where(lane < 64, in_low[48:112], in_high[0:64]),
        jnp.where(lane < 64, in_low[0:64], in_high[48:112]),
    )
    xbuf[c, v, 0:112] = chunk[0].astype(BF16)
    xbuf[c, v, 112:224] = chunk[1].astype(BF16)
    xbuf[c, v, 224:288] = packed.astype(BF16)

    def spread(pa, n):
        block = xbuf.at[c, v_of(pa, b)]
        for k, d in enumerate((2, 1, 3)):
            go(block, block, PB + 3 * n + k, plane_dev(0, d))
        go(block, block, SIB_X + n, sibling)

    mine = xbuf.at[c, v]
    for k, d in enumerate((1, 3, 2)):
        go(mine, mine, PA + k, plane_dev(d, 0))
    spread(a, 0)
    for k, d in enumerate((1, 3, 2)):
        pa = lax.rem(a + 4 - d, 4)
        arrive(xbuf.at[c, v_of(pa, b)], PA + k)
        spread(pa, k + 1)
    for n, d0 in enumerate((0, 1, 3, 2)):
        for k, d in enumerate((2, 1, 3)):
            block = xbuf.at[c, v_of(lax.rem(a + 4 - d0, 4), lax.rem(b + 4 - d, 4))]
            arrive(block, PB + 3 * n + k)
            go(block, block, SIB_X + 4 + 3 * n + k, sibling)
    for n, d0 in enumerate((0, 1, 3, 2)):
        pa = lax.rem(b + 4 - d0, 4)
        arrive(xbuf.at[o, v_sib(pa, a)], SIB_X + n)
    for n, d0 in enumerate((0, 1, 3, 2)):
        for k, d in enumerate((2, 1, 3)):
            pa, pb = lax.rem(b + 4 - d0, 4), lax.rem(a + 4 - d, 4)
            arrive(xbuf.at[o, v_sib(pa, pb)], SIB_X + 4 + 3 * n + k)
    heads[1].wait()

    nt = (((1,), (1,)), ((), ()))
    lane = iota((64, 128), 1)
    student = jnp.zeros((280, LIVE), F32)
    teacher = jnp.zeros((280, LIVE), F32)
    for u in range(8):
        even, odd_ = 2 * u, 2 * u + 1
        first, second = xbuf[0, even, 224:288].astype(F32), xbuf[0, odd_, 224:288].astype(F32)
        top = jnp.where(lane < 64, first, second)
        rest = pltpu.roll(jnp.where(lane < 64, second, first), 64, 1)[16:64]
        block = jnp.concatenate(
            [
                xbuf[0, even, 0:112], xbuf[0, even, 112:224],
                jnp.concatenate([top, rest], axis=0).astype(BF16),
                xbuf[0, odd_, 0:112], xbuf[0, odd_, 112:224],
            ],
            axis=1,
        )
        student += lax.dot_general(
            wst[:, 640 * u:640 * u + 640], block, nt, preferred_element_type=F32
        )
        block = jnp.concatenate(
            [
                xbuf[1, even, 0:112], xbuf[1, even, 112:224],
                xbuf[1, odd_, 0:112], xbuf[1, odd_, 112:224],
            ],
            axis=1,
        )
        teacher += lax.dot_general(
            wtt[:, 512 * u:512 * u + 512], block, nt, preferred_element_type=F32
        )
    zeros = jnp.zeros((280, 128 - LIVE), F32)
    student = jnp.concatenate([student, zeros], axis=1)
    teacher = jnp.concatenate([teacher, zeros], axis=1)
    diff = student - teacher
    peak_s = jnp.max(student, axis=0, keepdims=True)
    peak_t = jnp.max(teacher, axis=0, keepdims=True)
    expo = jnp.exp(student - peak_s)
    put_stats(st_a.at[c], (
        peak_s, peak_t,
        jnp.sum(expo, axis=0, keepdims=True),
        jnp.sum(jnp.exp(teacher - peak_t), axis=0, keepdims=True),
        jnp.sum(expo * diff, axis=0, keepdims=True),
    ))

    go(st_a.at[c], st_a.at[c], SIB_ST, sibling)
    arrive(st_a.at[o], SIB_ST)
    chip = merge(st_a[...])
    put_stats(st_b.at[v], chip)
    for n, (da, db) in enumerate(plane):
        go(st_b.at[v], st_b.at[v], PST + n, plane_dev(da, db))

    mass = expo * jnp.exp(peak_s - chip[0])
    g2[c, 0:280, 0:128] = (mass * (diff - chip[4] / chip[2])).astype(BF16)
    g2[c, 0:280, 128:256] = mass.astype(BF16)
    go(g2.at[c], g2.at[c], SIB_G, sibling)
    arrive(g2.at[o], SIB_G)

    def products(d):
        pb = lax.rem(b + d, 4)
        for pa in range(4):
            w = v_of(pa, pb)
            total = jnp.dot(wh[c, w], g2[c, 0:280], preferred_element_type=F32)
            total += jnp.dot(wsib[w], g2[o, 0:280], preferred_element_type=F32)
            if d:
                sb2[d - 1, pa] = total.astype(BF16)
            else:
                acc2[pa] = total

    for d in (2, 1, 3):
        products(d)
        go(sb2.at[d - 1], rb2.at[d - 1], R2 + d - 1, plane_dev(0, d))
    for n, (da, db) in enumerate(plane):
        arrive(st_b.at[v_of(lax.rem(a + 4 - da, 4), lax.rem(b + 4 - db, 4))], PST + n)
    put_stats(st_c.at[z], merge(st_b[...]))
    for n, d in enumerate(Z_ORDER):
        go(st_c.at[z], st_c.at[z], ZST + n, z_dev(d))
    products(0)
    for d in (1, 3, 2):
        arrive(rb2.at[d - 1], R2 + d - 1)
    for n, d in enumerate(Z_ORDER):
        arrive(st_c.at[lax.rem(z + 16 - d, 16)], ZST + n)
    peak_s, peak_t, sum_s, sum_t, cross = merge(st_c[...])
    lse_s = peak_s + jnp.log(sum_s)
    lse_t = peak_t + jnp.log(sum_t)
    divergence = cross / sum_s - lse_s + lse_t
    loss = as_col(weight * divergence, 128)
    ours = iota((1, 32), 1) == r
    start = jnp.sum(jnp.where(ours, before_row, 0.0), axis=1, keepdims=True)
    count = jnp.sum(jnp.where(ours, live_row, 0.0), axis=1, keepdims=True)
    slot = iota((1, 128), 1).astype(F32)
    at = jnp.where(slot < count, start + slot, -1.0).astype(jnp.int32)
    loss_ref[...] = jnp.sum(
        jnp.where(iota((128, 128), 0) == at, loss, 0.0), axis=0, keepdims=True
    )
    mean = cross / sum_s
    scales, shifts = [], []
    for d in range(4):
        shard = st_b[v_of(a, lax.rem(b + 4 - d, 4))]
        scales.append(weight * jnp.exp(shard[0:1] - peak_s) / sum_s)
        shifts.append(shard[4:5] / shard[2:3] - mean)
    for d in (2, 1, 3, 0):
        pa = lax.rem(a + d, 4)
        term = acc2[pa]
        total = scales[0] * (term[:, 0:128] + shifts[0] * term[:, 128:256])
        for k in range(3):
            term = rb2[k, pa].astype(F32)
            total += scales[k + 1] * (term[:, 0:128] + shifts[k + 1] * term[:, 128:256])
        if d:
            sb3[d - 1] = total.astype(BF16)
            go(sb3.at[d - 1], rb3.at[d - 1], R3 + d - 1, plane_dev(d, 0))
    for d in (1, 3, 2):
        arrive(rb3.at[d - 1], R3 + d - 1)
        total += rb3[d - 1].astype(F32)
    total = total.astype(BF16)

    place[...] = jnp.zeros_like(place)
    for k in range(4):
        place[k, 32 * k:32 * k + 32] = total[128:160]
    nt = (((1,), (1,)), ((), ()))
    spread_out = lax.dot_general(un1[...], total[0:128], nt, preferred_element_type=F32)
    for k in range(4):
        spread_out += lax.dot_general(un2[k], place[k], nt, preferred_element_type=F32)
    sb4[...] = spread_out.astype(BF16).reshape(16, 16, 128)
    rb4[z] = sb4[z]
    for n, d in enumerate(Z_ORDER):
        go(sb4.at[lax.rem(z + d, 16)], rb4.at[z], ZR + n, z_dev(d))
    for n, d in enumerate(Z_ORDER):
        arrive(rb4.at[lax.rem(z + 16 - d, 16)], ZR + n)
    full = jnp.sum(rb4[...].astype(F32), axis=0)
    sb5[c] = full
    go(sb5.at[c], sb5.at[c], SIB_R5, sibling)
    arrive(sb5.at[o], SIB_R5)
    grads = []
    for h in range(2):
        block = sb5[h]
        for row in range(12):
            at = 32 * (row % 4)
            tail[h, row:row + 1, 0:32] = block[12 + row // 4:13 + row // 4, at:at + 32]
        grads.append(jnp.where(c == 0, block[0:6], block[6:12]))
        grads.append(jnp.where(c == 0, tail[h, 0:6], tail[h, 6:12])[:, 0:32])
    grad_ref[:, 0:128] = grads[0]
    grad_ref[:, 128:160] = grads[1]
    grad_ref[:, 160:288] = grads[2]
    grad_ref[:, 288:320] = grads[3]
    for copy in pending:
        copy.wait_send()


def on_device(
    student_hidden, teacher_hidden, student_head, teacher_head,
    teacher_row, live_counts, branch_id, branch_ratio,
):
    vmem = pl.BlockSpec(memory_space=pltpu.VMEM)
    hbm = pl.BlockSpec(memory_space=pl.ANY)
    loss, grad = pl.pallas_call(
        kernel,
        out_shape=(
            jax.ShapeDtypeStruct((1, 128), F32),
            jax.ShapeDtypeStruct((6, 320), F32),
        ),
        in_specs=[hbm] * 8,
        out_specs=(vmem, vmem),
        scratch_shapes=[
            pltpu.VMEM((6, 320), BF16),
            pltpu.VMEM((6, 256), BF16),
            pltpu.VMEM((1, 192), jnp.int32),
            pltpu.VMEM((1, 32), jnp.int32),
            pltpu.VMEM((1, 192), jnp.int32),
            pltpu.VMEM((1, 16), F32),
            pltpu.VMEM((280, 5120), BF16),
            pltpu.VMEM((280, 4096), BF16),
            pltpu.VMEM((2, 16, 160, 280), BF16),
            pltpu.VMEM((16, 160, 280), BF16),
            pltpu.VMEM((8, 384), F32),
            pltpu.VMEM((2, 16, 128), BF16),
            pltpu.VMEM((16, 2, 16, 128), BF16),
            pltpu.VMEM((3, LIVE, 512), BF16),
            pltpu.VMEM((2, 16, HALF, 128), BF16),
            pltpu.VMEM((256, 128), BF16),
            pltpu.VMEM((4, 256, 128), BF16),
            pltpu.VMEM((2, 8, 128), F32),
            pltpu.VMEM((16, 8, 128), F32),
            pltpu.VMEM((16, 8, 128), F32),
            pltpu.VMEM((2, 288, 256), BF16),
            pltpu.VMEM((3, 4, 160, 256), BF16),
            pltpu.VMEM((3, 4, 160, 256), BF16),
            pltpu.VMEM((4, 160, 256), F32),
            pltpu.VMEM((3, 160, 128), BF16),
            pltpu.VMEM((3, 160, 128), BF16),
            pltpu.VMEM((4, 128, 128), BF16),
            pltpu.VMEM((16, 16, 128), BF16),
            pltpu.VMEM((16, 16, 128), BF16),
            pltpu.VMEM((2, 16, 128), F32),
            pltpu.VMEM((2, 16, 128), F32),
            pltpu.SemaphoreType.DMA((2,)),
            pltpu.SemaphoreType.DMA((6,)),
            pltpu.SemaphoreType.DMA((N_SEMS,)),
            pltpu.SemaphoreType.DMA((N_SEMS,)),
        ],
        compiler_params=pltpu.CompilerParams(
            collective_id=0, has_side_effects=True, vmem_limit_bytes=60 * 1024 * 1024
        ),
    )(
        student_hidden, teacher_hidden, student_head.T, teacher_head.T,
        teacher_row.reshape(1, -1), live_counts.reshape(1, -1),
        branch_id.reshape(1, -1), branch_ratio.reshape(1, -1),
    )
    return loss[0, 0:6], grad


def solution(mesh):
    in_specs = (
        P("rows", "vocab"),
        P("rows", "vocab"),
        P(None, ("rows", "vocab")),
        P(None, ("rows", "vocab")),
        P(),
        P(),
        P(),
        P(),
    )
    out_specs = (P("rows"), P("rows", "vocab"))
    return jax.shard_map(
        on_device, mesh=mesh, in_specs=in_specs,
        out_specs=out_specs, check_vma=False,
    )
```

```python
import jax
import jax.numpy as jnp
from jax import lax
from jax.experimental import pallas as pl
from jax.experimental.pallas import tpu as pltpu
from jax.sharding import PartitionSpec as P

MESH = pl.DeviceIdType.MESH
F32 = jnp.float32
BF16 = jnp.bfloat16
LIVE = 112
HALF = 256

SIB_P, SIB_X, SIB_ST, SIB_W, SIB_G, SIB_R5 = 0, 1, 17, 18, 20, 21
ZP, ZST, ZR = 22, 37, 52
PA, PB, PST, R2, R3 = 67, 70, 82, 97, 100
N_SEMS = 103
Z_ORDER = (8, 7, 9, 6, 10, 5, 11, 4, 12, 3, 13, 2, 14, 1, 15)


def iota(shape, dim):
    return lax.broadcasted_iota(jnp.int32, shape, dim)


def sixth(n):
    return lax.shift_right_logical(n * 171, 10)


def as_col(row, n):
    eye = iota((n, n), 0) == iota((n, n), 1)
    return jnp.sum(jnp.where(eye, row, 0.0), axis=1, keepdims=True)


def as_row(col, n):
    eye = iota((n, n), 0) == iota((n, n), 1)
    return jnp.sum(jnp.where(eye, col, 0.0), axis=0, keepdims=True)


def merge(stats):
    part = [stats[:, k, :] for k in range(5)]
    peak_s = jnp.max(part[0], axis=0, keepdims=True)
    peak_t = jnp.max(part[1], axis=0, keepdims=True)
    scale_s = jnp.exp(part[0] - peak_s)
    scale_t = jnp.exp(part[1] - peak_t)
    sum_s = jnp.sum(scale_s * part[2], axis=0, keepdims=True)
    sum_t = jnp.sum(scale_t * part[3], axis=0, keepdims=True)
    cross = jnp.sum(scale_s * part[4], axis=0, keepdims=True)
    return peak_s, peak_t, sum_s, sum_t, cross


def put_stats(ref, parts):
    row = iota((8, 128), 0)
    out = jnp.zeros((8, 128), F32)
    for k, part in enumerate(parts):
        out = jnp.where(row == k, part, out)
    ref[...] = out


def kernel(
    sh_hbm, th_hbm, ws_hbm, wt_hbm, trow_hbm, live_hbm, branch_hbm, ratio_hbm,
    loss_ref, grad_ref,
    sh_ref, th_ref, trow_ref, live_ref, branch_ref, ratio_ref,
    wst, wtt, wh, wsib, wide, parts, zbuf, sel, xbuf, un, st_a, st_b, st_c,
    g2, sb2, rb2, acc2, sb3, rb3, place, sb4, rb4, sb5, tail,
    head_sem, small_sem, send, recv,
):
    r = lax.axis_index("rows")
    v = lax.axis_index("vocab")
    z = lax.div(r, 2)
    c = lax.rem(r, 2)
    x = lax.div(v, 4)
    y = lax.rem(v, 4)
    o = 1 - c
    a = x * o + y * c
    b = y * o + x * c

    def v_of(pa, pb):
        return (pa * 4 + pb) * o + (pb * 4 + pa) * c

    def v_sib(pa, pb):
        return (pa * 4 + pb) * c + (pb * 4 + pa) * o

    sibling = (z * 2 + o, v)

    def z_dev(d):
        return (lax.rem(z + d, 16) * 2 + c, v)

    def plane_dev(da, db):
        return (r, v_of(lax.rem(a + da, 4), lax.rem(b + db, 4)))

    def rcopy(src, dst, number, device):
        return pltpu.make_async_remote_copy(
            src_ref=src, dst_ref=dst, send_sem=send.at[number], recv_sem=recv.at[number],
            device_id=device, device_id_type=MESH,
        )

    pending = []

    def go(src, dst, number, device):
        copy = rcopy(src, dst, number, device)
        copy.start()
        pending.append(copy)

    def arrive(dst, number):
        rcopy(dst, dst, number, sibling).wait_recv()

    heads = [
        pltpu.make_async_copy(ws_hbm, wst, head_sem.at[0]),
        pltpu.make_async_copy(wt_hbm, wtt, head_sem.at[1]),
    ]
    small = [
        pltpu.make_async_copy(src, dst, small_sem.at[n])
        for n, (src, dst) in enumerate((
            (sh_hbm, sh_ref), (th_hbm, th_ref), (trow_hbm, trow_ref),
            (live_hbm, live_ref), (branch_hbm, branch_ref), (ratio_hbm, ratio_ref),
        ))
    ]
    for copy in small + heads:
        copy.start()

    plane = [(da, db) for da in range(4) for db in range(4) if (da, db) != (0, 0)]
    plane.sort(key=lambda at: -min(at[0], 4 - at[0]) - min(at[1], 4 - at[1]))
    barrier = pltpu.get_barrier_semaphore()
    for d in Z_ORDER:
        pl.semaphore_signal(barrier, inc=1, device_id=z_dev(d), device_id_type=MESH)
    for da, db in plane:
        pl.semaphore_signal(barrier, inc=1, device_id=plane_dev(da, db), device_id_type=MESH)
    pl.semaphore_signal(barrier, inc=1, device_id=sibling, device_id_type=MESH)
    for copy in small:
        copy.wait()

    row16 = iota((16, 128), 0)
    wide[...] = jnp.zeros_like(wide)
    wide[0:6, 0:320] = sh_ref[...].astype(F32)
    sw = wide[...]
    odd = lax.rem(v, 2) == 1
    sw_odd = jnp.concatenate([pltpu.roll(sw, 320, 1)[:, 0:256], sw[:, 0:128]], axis=1)
    sw = jnp.where(odd, sw_odd, sw)
    s2 = jnp.where(iota((8, 128), 1) < 64, sw[:, 256:384], 0.0)
    s2_high = pltpu.roll(s2, 64, 1)
    th = th_ref[...].astype(F32)
    pack_s = jnp.zeros((16, 128), F32)
    pack_t = jnp.zeros((16, 128), F32)
    for i in range(6):
        pack_s = jnp.where(row16 == i, sw[i:i + 1, 0:128], pack_s)
        pack_s = jnp.where(row16 == 6 + i, sw[i:i + 1, 128:256], pack_s)
        pack_t = jnp.where(row16 == i, th[i:i + 1, 0:128], pack_t)
        pack_t = jnp.where(row16 == 6 + i, th[i:i + 1, 128:256], pack_t)
    for i in range(3):
        both = s2[i:i + 1, :] + s2_high[i + 3:i + 4, :]
        pack_s = jnp.where(row16 == 12 + i, both, pack_s)
        pack_t = jnp.where(row16 == 12 + i, both, pack_t)
    parts[0] = pack_s.astype(BF16)
    parts[1] = pack_t.astype(BF16)
    zbuf[z, c] = parts[c]

    live_row = live_ref[...].astype(F32)
    live_col = as_col(live_row, 32)
    owner_a, owner_b = iota((32, 32), 0), iota((32, 32), 1)
    before_col = jnp.sum(jnp.where(owner_b < owner_a, live_row, 0.0), axis=1, keepdims=True)
    before_row = jnp.sum(jnp.where(owner_a < owner_b, live_col, 0.0), axis=0, keepdims=True)
    pos = iota((1, 192), 1)
    pos_owner = sixth(pos)
    pos_slot = (pos - 6 * pos_owner).astype(F32)
    own = iota((32, 192), 0) == sixth(iota((32, 192), 1))
    rank = jnp.sum(jnp.where(own, before_col, 0.0), axis=0, keepdims=True) + pos_slot
    alive = jnp.sum(jnp.where(own, live_col, 0.0), axis=0, keepdims=True) > pos_slot
    rank = jnp.where(alive, rank, -1.0).astype(jnp.int32)
    pick = iota((128, 192), 0) == rank
    pos_of = jnp.sum(jnp.where(pick, pos.astype(F32), 0.0), axis=1, keepdims=True)
    teacher_of = jnp.sum(jnp.where(pick, trow_ref[...].astype(F32), 0.0), axis=1, keepdims=True)
    ratio_col = as_col(ratio_ref[...], 16)
    ratio_of = jnp.sum(
        jnp.where(iota((16, 192), 0) == branch_ref[...], ratio_col, 0.0), axis=0, keepdims=True
    )
    weight = as_row(jnp.sum(jnp.where(pick, ratio_of, 0.0), axis=1, keepdims=True), 128)
    def origin(source):
        owner = sixth(source)
        at_z = lax.shift_right_logical(owner, 1)
        return at_z * 32 + jnp.bitwise_and(owner, 1) * 16, source - 6 * owner

    pos_of = pos_of.astype(jnp.int32)[0:LIVE]
    base, src_slot = origin(jnp.where(c == 0, pos_of, teacher_of.astype(jnp.int32)[0:LIVE]))
    base_s, slot_s = origin(pos_of)
    low = slot_s < 3
    column = iota((LIVE, 512), 1)
    for k, at in enumerate((
        base + src_slot, base + 6 + src_slot, base_s + 12 + jnp.where(low, slot_s, slot_s - 3)
    )):
        sel[k] = jnp.where(column == at, 1.0, 0.0).astype(BF16)

    dest = iota((256, 1), 0)
    dest_z, q = lax.shift_right_logical(dest, 4), jnp.bitwise_and(dest, 15)

    def back(row, wanted):
        second = jnp.where(row >= 6, 1, 0)
        owner = 2 * dest_z + second
        slot = (row - 6 * second).astype(F32)
        mine = iota((256, 32), 1) == owner
        start = jnp.sum(jnp.where(mine, before_row, 0.0), axis=1, keepdims=True)
        count = jnp.sum(jnp.where(mine, live_row, 0.0), axis=1, keepdims=True)
        j = jnp.where(wanted & (slot < count), start + slot, -1.0).astype(jnp.int32)
        return jnp.where(iota((256, 128), 1) == j, 1.0, 0.0).astype(BF16)

    place[...] = jnp.zeros_like(place)
    un[:, 0:128] = back(q, q < 12)
    for g in range(4):
        un[:, 128 * g + 128:128 * g + 256] = back((q - 12) * 4 + g, (q >= 12) & (q < 15))

    pl.semaphore_wait(barrier, 31)
    go(parts.at[o], zbuf.at[z, c], SIB_P, sibling)
    arrive(zbuf.at[z, o], SIB_P)
    for n, d in enumerate(Z_ORDER):
        go(zbuf.at[z], zbuf.at[z], ZP + n, z_dev(d))

    def turn(part):
        for u in range(4 * part, 4 * part + 4):
            turned = jnp.transpose(wst[:, 640 * u:640 * u + 640])
            for k in range(4):
                wh[k % 2, 2 * u + k // 2] = turned[160 * k:160 * k + 160]
        where = pl.ds(8 * part, 8)
        go(wh.at[o, where], wsib.at[where], SIB_W + part, sibling)

    heads[0].wait()
    turn(0)
    for n, d in enumerate(Z_ORDER):
        arrive(zbuf.at[lax.rem(z + 16 - d, 16)], ZP + n)
    raw = zbuf[...].reshape(512, 128)
    chunk = [jnp.dot(sel[k], raw, preferred_element_type=F32) for k in range(3)]
    turned = pltpu.roll(chunk[2], 64, 1)
    lane = iota((64, 128), 1)
    in_low, in_high = jnp.where(low, chunk[2], turned), jnp.where(low, turned, chunk[2])
    packed = jnp.where(
        odd,
        jnp.where(lane < 64, in_low[48:112], in_high[0:64]),
        jnp.where(lane < 64, in_low[0:64], in_high[48:112]),
    )
    xbuf[c, v, 0:112] = chunk[0].astype(BF16)
    xbuf[c, v, 112:224] = chunk[1].astype(BF16)
    xbuf[c, v, 224:256] = jnp.where(c == 0, packed[0:32], packed[32:64]).astype(BF16)

    def spread(pa, n):
        block = xbuf.at[c, v_of(pa, b)]
        for k, d in enumerate((2, 1, 3)):
            go(block, block, PB + 3 * n + k, plane_dev(0, d))
        go(block, block, SIB_X + n, sibling)

    mine = xbuf.at[c, v]
    for k, d in enumerate((1, 3, 2)):
        go(mine, mine, PA + k, plane_dev(d, 0))
    spread(a, 0)
    turn(1)
    for k, d in enumerate((1, 3, 2)):
        pa = lax.rem(a + 4 - d, 4)
        arrive(xbuf.at[c, v_of(pa, b)], PA + k)
        spread(pa, k + 1)
    heads[1].wait()
    nt = (((1,), (1,)), ((), ()))
    student = jnp.zeros((280, LIVE), F32)
    teacher = jnp.zeros((280, LIVE), F32)

    def rows_of(part, w):
        return jnp.concatenate([xbuf[part, w, 0:112], xbuf[part, w, 112:224]], axis=1)

    def come(n, d0):
        for k, d in enumerate((2, 1, 3)):
            block = xbuf.at[c, v_of(lax.rem(a + 4 - d0, 4), lax.rem(b + 4 - d, 4))]
            arrive(block, PB + 3 * n + k)
            go(block, block, SIB_X + 4 + 3 * n + k, sibling)

    def come_over(n, d0):
        pa = lax.rem(b + 4 - d0, 4)
        arrive(xbuf.at[o, v_sib(pa, a)], SIB_X + n)
        for k, d in enumerate((2, 1, 3)):
            arrive(xbuf.at[o, v_sib(pa, lax.rem(a + 4 - d, 4))], SIB_X + 4 + 3 * n + k)

    def logits_of(student, teacher, d0):
        at = lax.rem(x + 4 - d0, 4)
        left = [
            wst[:, pl.ds(pl.multiple_of(1280 * at + begin, 128), 256)] for begin in (0, 384, 640, 1024)
        ]
        right = [rows_of(0, 4 * at + k) for k in range(4)]
        student += lax.dot_general(
            jnp.concatenate(left, axis=1), jnp.concatenate(right, axis=1), nt,
            preferred_element_type=F32,
        )
        at = lax.rem(y + 4 - d0, 4)
        left = [wtt[:, pl.ds(pl.multiple_of(1024 * k + 256 * at, 128), 256)] for k in range(4)]
        right = [rows_of(1, 4 * k + at) for k in range(4)]
        teacher += lax.dot_general(
            jnp.concatenate(left, axis=1), jnp.concatenate(right, axis=1), nt,
            preferred_element_type=F32,
        )
        return student, teacher

    places = (0, 1, 3, 2)
    for n, d0 in enumerate(places):
        come(n, d0)
        if n:
            come_over(n - 1, places[n - 1])
            student, teacher = logits_of(student, teacher, places[n - 1])
    come_over(3, places[3])
    for part in range(2):
        where = pl.ds(8 * part, 8)
        arrive(wsib.at[where], SIB_W + part)
    student, teacher = logits_of(student, teacher, places[3])
    lane = iota((64, 128), 1)
    for part in range(2):
        left, right = [], []
        for u in range(4 * part, 4 * part + 4):
            first, second = [
                jnp.concatenate([xbuf[0, w, 224:256], xbuf[1, w, 224:256]], axis=0).astype(F32)
                for w in (2 * u, 2 * u + 1)
            ]
            top = jnp.where(lane < 64, first, second)
            rest = pltpu.roll(jnp.where(lane < 64, second, first), 64, 1)[16:64]
            left.append(wst[:, 640 * u + 256:640 * u + 384])
            right.append(jnp.concatenate([top, rest], axis=0).astype(BF16))
        student += lax.dot_general(
            jnp.concatenate(left, axis=1), jnp.concatenate(right, axis=1), nt,
            preferred_element_type=F32,
        )
    zeros = jnp.zeros((280, 128 - LIVE), F32)
    student = jnp.concatenate([student, zeros], axis=1)
    teacher = jnp.concatenate([teacher, zeros], axis=1)
    diff = student - teacher
    peak_s = jnp.max(student, axis=0, keepdims=True)
    peak_t = jnp.max(teacher, axis=0, keepdims=True)
    expo = jnp.exp(student - peak_s)
    put_stats(st_a.at[c], (
        peak_s, peak_t,
        jnp.sum(expo, axis=0, keepdims=True),
        jnp.sum(jnp.exp(teacher - peak_t), axis=0, keepdims=True),
        jnp.sum(expo * diff, axis=0, keepdims=True),
    ))

    go(st_a.at[c], st_a.at[c], SIB_ST, sibling)
    arrive(st_a.at[o], SIB_ST)
    chip = merge(st_a[...])
    mass = expo * jnp.exp(peak_s - chip[0])
    g2[c, 0:280, 0:128] = (mass * (diff - chip[4] / chip[2])).astype(BF16)
    g2[c, 0:280, 128:256] = mass.astype(BF16)
    go(g2.at[c], g2.at[c], SIB_G, sibling)
    put_stats(st_b.at[v], chip)
    for n, (da, db) in enumerate(plane):
        go(st_b.at[v], st_b.at[v], PST + n, plane_dev(da, db))
    arrive(g2.at[o], SIB_G)

    def products(d):
        places_here = [v_of(pa, lax.rem(b + d, 4)) for pa in range(4)]
        total = jnp.dot(
            jnp.concatenate([wh[c, w] for w in places_here], axis=0), g2[c, 0:280],
            preferred_element_type=F32,
        )
        total += jnp.dot(
            jnp.concatenate([wsib[w] for w in places_here], axis=0), g2[o, 0:280],
            preferred_element_type=F32,
        )
        if d:
            sb2[d - 1] = total.astype(BF16).reshape(4, 160, 256)
        else:
            acc2[...] = total.reshape(4, 160, 256)

    for d in (2, 1, 3):
        products(d)
        go(sb2.at[d - 1], rb2.at[d - 1], R2 + d - 1, plane_dev(0, d))
    for n, (da, db) in enumerate(plane):
        arrive(st_b.at[v_of(lax.rem(a + 4 - da, 4), lax.rem(b + 4 - db, 4))], PST + n)
    put_stats(st_c.at[z], merge(st_b[...]))
    for n, d in enumerate(Z_ORDER):
        go(st_c.at[z], st_c.at[z], ZST + n, z_dev(d))
    products(0)
    for d in (1, 3, 2):
        arrive(rb2.at[d - 1], R2 + d - 1)
    for n, d in enumerate(Z_ORDER):
        arrive(st_c.at[lax.rem(z + 16 - d, 16)], ZST + n)
    peak_s, peak_t, sum_s, sum_t, cross = merge(st_c[...])
    lse_s = peak_s + jnp.log(sum_s)
    lse_t = peak_t + jnp.log(sum_t)
    divergence = cross / sum_s - lse_s + lse_t
    loss = as_col(weight * divergence, 128)
    ours = iota((1, 32), 1) == r
    start = jnp.sum(jnp.where(ours, before_row, 0.0), axis=1, keepdims=True)
    count = jnp.sum(jnp.where(ours, live_row, 0.0), axis=1, keepdims=True)
    slot = iota((1, 128), 1).astype(F32)
    at = jnp.where(slot < count, start + slot, -1.0).astype(jnp.int32)
    loss_ref[...] = jnp.sum(
        jnp.where(iota((128, 128), 0) == at, loss, 0.0), axis=0, keepdims=True
    )
    mean = cross / sum_s
    scales, shifts = [], []
    for d in range(4):
        shard = st_b[v_of(a, lax.rem(b + 4 - d, 4))]
        scales.append(weight * jnp.exp(shard[0:1] - peak_s) / sum_s)
        shifts.append(shard[4:5] / shard[2:3] - mean)
    for d in (2, 1, 3, 0):
        pa = lax.rem(a + d, 4)
        term = acc2[pa]
        total = scales[0] * (term[:, 0:128] + shifts[0] * term[:, 128:256])
        for k in range(3):
            term = rb2[k, pa].astype(F32)
            total += scales[k + 1] * (term[:, 0:128] + shifts[k + 1] * term[:, 128:256])
        if d:
            sb3[d - 1] = total.astype(BF16)
            go(sb3.at[d - 1], rb3.at[d - 1], R3 + d - 1, plane_dev(d, 0))
    for d in (1, 3, 2):
        arrive(rb3.at[d - 1], R3 + d - 1)
        total += rb3[d - 1].astype(F32)
    total = total.astype(BF16)

    place[:, 0:128] = total[0:128]
    for k in range(4):
        place[32 * k:32 * k + 32, 128 * k + 128:128 * k + 256] = total[128:160]
    spread_out = lax.dot_general(un[...], place[...], nt, preferred_element_type=F32)
    sb4[...] = spread_out.astype(BF16).reshape(16, 16, 128)
    rb4[z] = sb4[z]
    for n, d in enumerate(Z_ORDER):
        go(sb4.at[lax.rem(z + d, 16)], rb4.at[z], ZR + n, z_dev(d))
    for n, d in enumerate(Z_ORDER):
        arrive(rb4.at[lax.rem(z + 16 - d, 16)], ZR + n)
    full = jnp.sum(rb4[...].astype(F32), axis=0)
    sb5[c] = full
    go(sb5.at[c], sb5.at[c], SIB_R5, sibling)

    def ends(h, block):
        for row in range(12):
            at = 32 * (row % 4)
            tail[h, row:row + 1, 0:32] = block[12 + row // 4:13 + row // 4, at:at + 32]

    ends(c, full)
    arrive(sb5.at[o], SIB_R5)
    ends(o, sb5[o])
    grads = []
    for h in range(2):
        block = sb5[h]
        grads.append(jnp.where(c == 0, block[0:6], block[6:12]))
        grads.append(jnp.where(c == 0, tail[h, 0:6], tail[h, 6:12])[:, 0:32])
    grad_ref[:, 0:128] = grads[0]
    grad_ref[:, 128:160] = grads[1]
    grad_ref[:, 160:288] = grads[2]
    grad_ref[:, 288:320] = grads[3]
    for copy in pending:
        copy.wait_send()


def on_device(
    student_hidden, teacher_hidden, student_head, teacher_head,
    teacher_row, live_counts, branch_id, branch_ratio,
):
    vmem = pl.BlockSpec(memory_space=pltpu.VMEM)
    hbm = pl.BlockSpec(memory_space=pl.ANY)
    loss, grad = pl.pallas_call(
        kernel,
        out_shape=(
            jax.ShapeDtypeStruct((1, 128), F32),
            jax.ShapeDtypeStruct((6, 320), F32),
        ),
        in_specs=[hbm] * 8,
        out_specs=(vmem, vmem),
        scratch_shapes=[
            pltpu.VMEM((6, 320), BF16),
            pltpu.VMEM((6, 256), BF16),
            pltpu.VMEM((1, 192), jnp.int32),
            pltpu.VMEM((1, 32), jnp.int32),
            pltpu.VMEM((1, 192), jnp.int32),
            pltpu.VMEM((1, 16), F32),
            pltpu.VMEM((280, 5120), BF16),
            pltpu.VMEM((280, 4096), BF16),
            pltpu.VMEM((2, 16, 160, 280), BF16),
            pltpu.VMEM((16, 160, 280), BF16),
            pltpu.VMEM((8, 384), F32),
            pltpu.VMEM((2, 16, 128), BF16),
            pltpu.VMEM((16, 2, 16, 128), BF16),
            pltpu.VMEM((3, LIVE, 512), BF16),
            pltpu.VMEM((2, 16, HALF, 128), BF16),
            pltpu.VMEM((256, 640), BF16),
            pltpu.VMEM((2, 8, 128), F32),
            pltpu.VMEM((16, 8, 128), F32),
            pltpu.VMEM((16, 8, 128), F32),
            pltpu.VMEM((2, 288, 256), BF16),
            pltpu.VMEM((3, 4, 160, 256), BF16),
            pltpu.VMEM((3, 4, 160, 256), BF16),
            pltpu.VMEM((4, 160, 256), F32),
            pltpu.VMEM((3, 160, 128), BF16),
            pltpu.VMEM((3, 160, 128), BF16),
            pltpu.VMEM((128, 640), BF16),
            pltpu.VMEM((16, 16, 128), BF16),
            pltpu.VMEM((16, 16, 128), BF16),
            pltpu.VMEM((2, 16, 128), F32),
            pltpu.VMEM((2, 16, 128), F32),
            pltpu.SemaphoreType.DMA((2,)),
            pltpu.SemaphoreType.DMA((6,)),
            pltpu.SemaphoreType.DMA((N_SEMS,)),
            pltpu.SemaphoreType.DMA((N_SEMS,)),
        ],
        compiler_params=pltpu.CompilerParams(
            collective_id=0, has_side_effects=True, vmem_limit_bytes=60 * 1024 * 1024
        ),
    )(
        student_hidden, teacher_hidden, student_head.T, teacher_head.T,
        teacher_row.reshape(1, -1), live_counts.reshape(1, -1),
        branch_id.reshape(1, -1), branch_ratio.reshape(1, -1),
    )
    return loss[0, 0:6], grad


def solution(mesh):
    in_specs = (
        P("rows", "vocab"),
        P("rows", "vocab"),
        P(None, ("rows", "vocab")),
        P(None, ("rows", "vocab")),
        P(),
        P(),
        P(),
        P(),
    )
    out_specs = (P("rows"), P("rows", "vocab"))
    return jax.shard_map(
        on_device, mesh=mesh, in_specs=in_specs,
        out_specs=out_specs, check_vma=False,
    )
```

```python
import jax
import jax.numpy as jnp
from jax import lax
from jax.experimental import pallas as pl
from jax.experimental.pallas import tpu as pltpu
from jax.sharding import PartitionSpec as P

MESH = pl.DeviceIdType.MESH
F32 = jnp.float32
BF16 = jnp.bfloat16
LIVE = 112
HALF = 256

SIB_P, SIB_X, SIB_ST, SIB_W, SIB_G, SIB_R5 = 0, 1, 17, 18, 20, 21
ZP, ZST, ZR = 22, 37, 52
PA, PB, PST, R2, R3 = 67, 70, 82, 97, 100
N_SEMS = 103
Z_ORDER = (8, 7, 9, 6, 10, 5, 11, 4, 12, 3, 13, 2, 14, 1, 15)


def iota(shape, dim):
    return lax.broadcasted_iota(jnp.int32, shape, dim)


def sixth(n):
    return lax.shift_right_logical(n * 171, 10)


def as_col(row, n):
    eye = iota((n, n), 0) == iota((n, n), 1)
    return jnp.sum(jnp.where(eye, row, 0.0), axis=1, keepdims=True)


def as_row(col, n):
    eye = iota((n, n), 0) == iota((n, n), 1)
    return jnp.sum(jnp.where(eye, col, 0.0), axis=0, keepdims=True)


def merge(stats):
    part = [stats[:, k, :] for k in range(5)]
    peak_s = jnp.max(part[0], axis=0, keepdims=True)
    peak_t = jnp.max(part[1], axis=0, keepdims=True)
    scale_s = jnp.exp(part[0] - peak_s)
    scale_t = jnp.exp(part[1] - peak_t)
    sum_s = jnp.sum(scale_s * part[2], axis=0, keepdims=True)
    sum_t = jnp.sum(scale_t * part[3], axis=0, keepdims=True)
    cross = jnp.sum(scale_s * part[4], axis=0, keepdims=True)
    return peak_s, peak_t, sum_s, sum_t, cross


def put_stats(ref, parts):
    row = iota((8, 128), 0)
    out = jnp.zeros((8, 128), F32)
    for k, part in enumerate(parts):
        out = jnp.where(row == k, part, out)
    ref[...] = out


def kernel(
    sh_hbm, th_hbm, ws_hbm, wt_hbm, trow_hbm, live_hbm, branch_hbm, ratio_hbm,
    loss_ref, grad_ref,
    sh_ref, th_ref, trow_ref, live_ref, branch_ref, ratio_ref,
    wst, wtt, wh, wsib, wide, parts, zbuf, sel, xbuf, un, st_a, st_b, st_c,
    g2, sb2, rb2, acc2, sb3, rb3, place, sb4, rb4, sb5, tail,
    head_sem, small_sem, send, recv,
):
    r = lax.axis_index("rows")
    v = lax.axis_index("vocab")
    z = lax.div(r, 2)
    c = lax.rem(r, 2)
    x = lax.div(v, 4)
    y = lax.rem(v, 4)
    o = 1 - c
    a = x * o + y * c
    b = y * o + x * c

    def v_of(pa, pb):
        return (pa * 4 + pb) * o + (pb * 4 + pa) * c

    def v_sib(pa, pb):
        return (pa * 4 + pb) * c + (pb * 4 + pa) * o

    sibling = (z * 2 + o, v)

    def z_dev(d):
        return (lax.rem(z + d, 16) * 2 + c, v)

    def plane_dev(da, db):
        return (r, v_of(lax.rem(a + da, 4), lax.rem(b + db, 4)))

    def rcopy(src, dst, number, device):
        return pltpu.make_async_remote_copy(
            src_ref=src, dst_ref=dst, send_sem=send.at[number], recv_sem=recv.at[number],
            device_id=device, device_id_type=MESH,
        )

    pending = []

    def go(src, dst, number, device):
        copy = rcopy(src, dst, number, device)
        copy.start()
        pending.append(copy)

    def arrive(dst, number):
        rcopy(dst, dst, number, sibling).wait_recv()

    heads = [
        pltpu.make_async_copy(ws_hbm, wst, head_sem.at[0]),
        pltpu.make_async_copy(wt_hbm, wtt, head_sem.at[1]),
    ]
    small = [
        pltpu.make_async_copy(src, dst, small_sem.at[n])
        for n, (src, dst) in enumerate((
            (sh_hbm, sh_ref), (th_hbm, th_ref), (trow_hbm, trow_ref),
            (live_hbm, live_ref), (branch_hbm, branch_ref), (ratio_hbm, ratio_ref),
        ))
    ]
    for copy in small + heads:
        copy.start()

    plane = [(da, db) for da in range(4) for db in range(4) if (da, db) != (0, 0)]
    plane.sort(key=lambda at: -min(at[0], 4 - at[0]) - min(at[1], 4 - at[1]))
    barrier = pltpu.get_barrier_semaphore()
    for d in Z_ORDER:
        pl.semaphore_signal(barrier, inc=1, device_id=z_dev(d), device_id_type=MESH)
    for da, db in plane:
        pl.semaphore_signal(barrier, inc=1, device_id=plane_dev(da, db), device_id_type=MESH)
    pl.semaphore_signal(barrier, inc=1, device_id=sibling, device_id_type=MESH)
    for copy in small:
        copy.wait()

    row16 = iota((16, 128), 0)
    wide[...] = jnp.zeros_like(wide)
    wide[0:6, 0:320] = sh_ref[...].astype(F32)
    sw = wide[...]
    odd = lax.rem(v, 2) == 1
    sw_odd = jnp.concatenate([pltpu.roll(sw, 320, 1)[:, 0:256], sw[:, 0:128]], axis=1)
    sw = jnp.where(odd, sw_odd, sw)
    s2 = jnp.where(iota((8, 128), 1) < 64, sw[:, 256:384], 0.0)
    s2_high = pltpu.roll(s2, 64, 1)
    th = th_ref[...].astype(F32)
    pack_s = jnp.zeros((16, 128), F32)
    pack_t = jnp.zeros((16, 128), F32)
    for i in range(6):
        pack_s = jnp.where(row16 == i, sw[i:i + 1, 0:128], pack_s)
        pack_s = jnp.where(row16 == 6 + i, sw[i:i + 1, 128:256], pack_s)
        pack_t = jnp.where(row16 == i, th[i:i + 1, 0:128], pack_t)
        pack_t = jnp.where(row16 == 6 + i, th[i:i + 1, 128:256], pack_t)
    for i in range(3):
        both = s2[i:i + 1, :] + s2_high[i + 3:i + 4, :]
        pack_s = jnp.where(row16 == 12 + i, both, pack_s)
        pack_t = jnp.where(row16 == 12 + i, both, pack_t)
    parts[0] = pack_s.astype(BF16)
    parts[1] = pack_t.astype(BF16)
    zbuf[z, c] = parts[c]

    live_row = live_ref[...].astype(F32)
    live_col = as_col(live_row, 32)
    owner_a, owner_b = iota((32, 32), 0), iota((32, 32), 1)
    before_col = jnp.sum(jnp.where(owner_b < owner_a, live_row, 0.0), axis=1, keepdims=True)
    before_row = jnp.sum(jnp.where(owner_a < owner_b, live_col, 0.0), axis=0, keepdims=True)
    pos = iota((1, 192), 1)
    pos_owner = sixth(pos)
    pos_slot = (pos - 6 * pos_owner).astype(F32)
    own = iota((32, 192), 0) == sixth(iota((32, 192), 1))
    rank = jnp.sum(jnp.where(own, before_col, 0.0), axis=0, keepdims=True) + pos_slot
    alive = jnp.sum(jnp.where(own, live_col, 0.0), axis=0, keepdims=True) > pos_slot
    rank = jnp.where(alive, rank, -1.0).astype(jnp.int32)
    pick = iota((128, 192), 0) == rank
    pos_of = jnp.sum(jnp.where(pick, pos.astype(F32), 0.0), axis=1, keepdims=True)
    teacher_of = jnp.sum(jnp.where(pick, trow_ref[...].astype(F32), 0.0), axis=1, keepdims=True)
    ratio_col = as_col(ratio_ref[...], 16)
    ratio_of = jnp.sum(
        jnp.where(iota((16, 192), 0) == branch_ref[...], ratio_col, 0.0), axis=0, keepdims=True
    )
    weight = as_row(jnp.sum(jnp.where(pick, ratio_of, 0.0), axis=1, keepdims=True), 128)
    def origin(source):
        owner = sixth(source)
        at_z = lax.shift_right_logical(owner, 1)
        return at_z * 32 + jnp.bitwise_and(owner, 1) * 16, source - 6 * owner

    pos_of = pos_of.astype(jnp.int32)[0:LIVE]
    base, src_slot = origin(jnp.where(c == 0, pos_of, teacher_of.astype(jnp.int32)[0:LIVE]))
    base_s, slot_s = origin(pos_of)
    low = slot_s < 3
    column = iota((LIVE, 512), 1)
    for k, at in enumerate((
        base + src_slot, base + 6 + src_slot, base_s + 12 + jnp.where(low, slot_s, slot_s - 3)
    )):
        sel[k] = jnp.where(column == at, 1.0, 0.0).astype(BF16)

    dest = iota((256, 1), 0)
    dest_z, q = lax.shift_right_logical(dest, 4), jnp.bitwise_and(dest, 15)

    def back(row, wanted):
        second = jnp.where(row >= 6, 1, 0)
        owner = 2 * dest_z + second
        slot = (row - 6 * second).astype(F32)
        mine = iota((256, 32), 1) == owner
        start = jnp.sum(jnp.where(mine, before_row, 0.0), axis=1, keepdims=True)
        count = jnp.sum(jnp.where(mine, live_row, 0.0), axis=1, keepdims=True)
        j = jnp.where(wanted & (slot < count), start + slot, -1.0).astype(jnp.int32)
        return jnp.where(iota((256, 128), 1) == j, 1.0, 0.0).astype(BF16)

    place[...] = jnp.zeros_like(place)
    un[:, 0:128] = back(q, q < 12)
    for g in range(4):
        un[:, 128 * g + 128:128 * g + 256] = back((q - 12) * 4 + g, (q >= 12) & (q < 15))

    pl.semaphore_wait(barrier, 31)
    go(parts.at[o], zbuf.at[z, c], SIB_P, sibling)
    arrive(zbuf.at[z, o], SIB_P)
    for n, d in enumerate(Z_ORDER):
        go(zbuf.at[z], zbuf.at[z], ZP + n, z_dev(d))

    def turn(part):
        for u in range(4 * part, 4 * part + 4):
            turned = jnp.transpose(wst[:, 640 * u:640 * u + 640])
            for k in range(4):
                wh[k % 2, 2 * u + k // 2] = turned[160 * k:160 * k + 160]
        where = pl.ds(8 * part, 8)
        go(wh.at[o, where], wsib.at[where], SIB_W + part, sibling)

    heads[0].wait()
    turn(0)
    for n, d in enumerate(Z_ORDER):
        arrive(zbuf.at[lax.rem(z + 16 - d, 16)], ZP + n)
    raw = zbuf[...].reshape(512, 128)
    chunk = [jnp.dot(sel[k], raw, preferred_element_type=F32) for k in range(3)]
    turned = pltpu.roll(chunk[2], 64, 1)
    lane = iota((64, 128), 1)
    in_low, in_high = jnp.where(low, chunk[2], turned), jnp.where(low, turned, chunk[2])
    packed = jnp.where(
        odd,
        jnp.where(lane < 64, in_low[48:112], in_high[0:64]),
        jnp.where(lane < 64, in_low[0:64], in_high[48:112]),
    )
    xbuf[c, v, 0:112] = chunk[0].astype(BF16)
    xbuf[c, v, 112:224] = chunk[1].astype(BF16)
    xbuf[c, v, 224:256] = jnp.where(c == 0, packed[0:32], packed[32:64]).astype(BF16)

    def spread(pa, n):
        block = xbuf.at[c, v_of(pa, b)]
        for k, d in enumerate((2, 1, 3)):
            go(block, block, PB + 3 * n + k, plane_dev(0, d))
        go(block, block, SIB_X + n, sibling)

    mine = xbuf.at[c, v]
    for k, d in enumerate((1, 3, 2)):
        go(mine, mine, PA + k, plane_dev(d, 0))
    spread(a, 0)
    turn(1)
    for k, d in enumerate((1, 3, 2)):
        pa = lax.rem(a + 4 - d, 4)
        arrive(xbuf.at[c, v_of(pa, b)], PA + k)
        spread(pa, k + 1)
    heads[1].wait()
    nt = (((1,), (1,)), ((), ()))
    student = jnp.zeros((280, LIVE), F32)
    teacher = jnp.zeros((280, LIVE), F32)

    def rows_of(part, w):
        return jnp.concatenate([xbuf[part, w, 0:112], xbuf[part, w, 112:224]], axis=1)

    def come(n, d0):
        for k, d in enumerate((2, 1, 3)):
            block = xbuf.at[c, v_of(lax.rem(a + 4 - d0, 4), lax.rem(b + 4 - d, 4))]
            arrive(block, PB + 3 * n + k)
            go(block, block, SIB_X + 4 + 3 * n + k, sibling)

    def come_over(n, d0):
        pa = lax.rem(b + 4 - d0, 4)
        arrive(xbuf.at[o, v_sib(pa, a)], SIB_X + n)
        for k, d in enumerate((2, 1, 3)):
            arrive(xbuf.at[o, v_sib(pa, lax.rem(a + 4 - d, 4))], SIB_X + 4 + 3 * n + k)

    def logits_of(student, teacher, d0):
        at = lax.rem(x + 4 - d0, 4)
        left = [
            wst[:, pl.ds(pl.multiple_of(1280 * at + begin, 128), 256)] for begin in (0, 384, 640, 1024)
        ]
        right = [rows_of(0, 4 * at + k) for k in range(4)]
        student += lax.dot_general(
            jnp.concatenate(left, axis=1), jnp.concatenate(right, axis=1), nt,
            preferred_element_type=F32,
        )
        at = lax.rem(y + 4 - d0, 4)
        left = [wtt[:, pl.ds(pl.multiple_of(1024 * k + 256 * at, 128), 256)] for k in range(4)]
        right = [rows_of(1, 4 * k + at) for k in range(4)]
        teacher += lax.dot_general(
            jnp.concatenate(left, axis=1), jnp.concatenate(right, axis=1), nt,
            preferred_element_type=F32,
        )
        return student, teacher

    places = (0, 1, 3, 2)
    for n, d0 in enumerate(places):
        come(n, d0)
        if n:
            come_over(n - 1, places[n - 1])
            student, teacher = logits_of(student, teacher, places[n - 1])
    come_over(3, places[3])
    for part in range(2):
        where = pl.ds(8 * part, 8)
        arrive(wsib.at[where], SIB_W + part)
    student, teacher = logits_of(student, teacher, places[3])
    lane = iota((64, 128), 1)
    for part in range(2):
        left, right = [], []
        for u in range(4 * part, 4 * part + 4):
            first, second = [
                jnp.concatenate([xbuf[0, w, 224:256], xbuf[1, w, 224:256]], axis=0).astype(F32)
                for w in (2 * u, 2 * u + 1)
            ]
            top = jnp.where(lane < 64, first, second)
            rest = pltpu.roll(jnp.where(lane < 64, second, first), 64, 1)[16:64]
            left.append(wst[:, 640 * u + 256:640 * u + 384])
            right.append(jnp.concatenate([top, rest], axis=0).astype(BF16))
        student += lax.dot_general(
            jnp.concatenate(left, axis=1), jnp.concatenate(right, axis=1), nt,
            preferred_element_type=F32,
        )
    zeros = jnp.zeros((280, 128 - LIVE), F32)
    student = jnp.concatenate([student, zeros], axis=1)
    teacher = jnp.concatenate([teacher, zeros], axis=1)
    diff = student - teacher
    peak_s = jnp.max(student, axis=0, keepdims=True)
    peak_t = jnp.max(teacher, axis=0, keepdims=True)
    expo = jnp.exp(student - peak_s)
    put_stats(st_a.at[c], (
        peak_s, peak_t,
        jnp.sum(expo, axis=0, keepdims=True),
        jnp.sum(jnp.exp(teacher - peak_t), axis=0, keepdims=True),
        jnp.sum(expo * diff, axis=0, keepdims=True),
    ))

    go(st_a.at[c], st_a.at[c], SIB_ST, sibling)
    arrive(st_a.at[o], SIB_ST)
    chip = merge(st_a[...])
    mass = expo * jnp.exp(peak_s - chip[0])
    g2[c, 0:280, 0:128] = (mass * (diff - chip[4] / chip[2])).astype(BF16)
    g2[c, 0:280, 128:256] = mass.astype(BF16)
    go(g2.at[c], g2.at[c], SIB_G, sibling)
    put_stats(st_b.at[v], chip)
    for n, (da, db) in enumerate(plane):
        go(st_b.at[v], st_b.at[v], PST + n, plane_dev(da, db))
    arrive(g2.at[o], SIB_G)

    def products(d):
        places_here = [v_of(pa, lax.rem(b + d, 4)) for pa in range(4)]
        total = jnp.dot(
            jnp.concatenate([wh[c, w] for w in places_here], axis=0), g2[c, 0:280],
            preferred_element_type=F32,
        )
        total += jnp.dot(
            jnp.concatenate([wsib[w] for w in places_here], axis=0), g2[o, 0:280],
            preferred_element_type=F32,
        )
        if d:
            sb2[d - 1] = total.astype(BF16).reshape(4, 160, 256)
        else:
            acc2[...] = total.reshape(4, 160, 256)

    for d in (2, 1, 3):
        products(d)
        go(sb2.at[d - 1], rb2.at[d - 1], R2 + d - 1, plane_dev(0, d))
    for n, (da, db) in enumerate(plane):
        arrive(st_b.at[v_of(lax.rem(a + 4 - da, 4), lax.rem(b + 4 - db, 4))], PST + n)
    put_stats(st_c.at[z], merge(st_b[...]))
    for n, d in enumerate(Z_ORDER):
        go(st_c.at[z], st_c.at[z], ZST + n, z_dev(d))
    products(0)
    for d in (1, 3, 2):
        arrive(rb2.at[d - 1], R2 + d - 1)
    for n, d in enumerate(Z_ORDER):
        arrive(st_c.at[lax.rem(z + 16 - d, 16)], ZST + n)
    peak_s, peak_t, sum_s, sum_t, cross = merge(st_c[...])
    lse_s = peak_s + jnp.log(sum_s)
    lse_t = peak_t + jnp.log(sum_t)
    divergence = cross / sum_s - lse_s + lse_t
    loss = as_col(weight * divergence, 128)
    ours = iota((1, 32), 1) == r
    start = jnp.sum(jnp.where(ours, before_row, 0.0), axis=1, keepdims=True)
    count = jnp.sum(jnp.where(ours, live_row, 0.0), axis=1, keepdims=True)
    slot = iota((1, 128), 1).astype(F32)
    at = jnp.where(slot < count, start + slot, -1.0).astype(jnp.int32)
    loss_ref[...] = jnp.sum(
        jnp.where(iota((128, 128), 0) == at, loss, 0.0), axis=0, keepdims=True
    )[:, 0:6]
    mean = cross / sum_s
    scales, shifts = [], []
    for d in range(4):
        shard = st_b[v_of(a, lax.rem(b + 4 - d, 4))]
        scales.append(weight * jnp.exp(shard[0:1] - peak_s) / sum_s)
        shifts.append(shard[4:5] / shard[2:3] - mean)
    for d in (2, 1, 3, 0):
        pa = lax.rem(a + d, 4)
        term = acc2[pa]
        total = scales[0] * (term[:, 0:128] + shifts[0] * term[:, 128:256])
        for k in range(3):
            term = rb2[k, pa].astype(F32)
            total += scales[k + 1] * (term[:, 0:128] + shifts[k + 1] * term[:, 128:256])
        if d:
            sb3[d - 1] = total.astype(BF16)
            go(sb3.at[d - 1], rb3.at[d - 1], R3 + d - 1, plane_dev(d, 0))
    for d in (1, 3, 2):
        arrive(rb3.at[d - 1], R3 + d - 1)
        total += rb3[d - 1].astype(F32)
    total = total.astype(BF16)

    place[:, 0:128] = total[0:128]
    for k in range(4):
        place[32 * k:32 * k + 32, 128 * k + 128:128 * k + 256] = total[128:160]
    spread_out = lax.dot_general(un[...], place[...], nt, preferred_element_type=F32)
    sb4[...] = spread_out.astype(BF16).reshape(16, 16, 128)
    rb4[z] = sb4[z]
    for n, d in enumerate(Z_ORDER):
        go(sb4.at[lax.rem(z + d, 16)], rb4.at[z], ZR + n, z_dev(d))
    for n, d in enumerate(Z_ORDER):
        arrive(rb4.at[lax.rem(z + 16 - d, 16)], ZR + n)
    full = jnp.sum(rb4[...].astype(F32), axis=0)
    sb5[c] = full
    go(sb5.at[c], sb5.at[c], SIB_R5, sibling)

    def ends(h, block):
        for row in range(12):
            at = 32 * (row % 4)
            tail[h, row:row + 1, 0:32] = block[12 + row // 4:13 + row // 4, at:at + 32]

    ends(c, full)
    arrive(sb5.at[o], SIB_R5)
    ends(o, sb5[o])
    grads = []
    for h in range(2):
        block = sb5[h]
        grads.append(jnp.where(c == 0, block[0:6], block[6:12]))
        grads.append(jnp.where(c == 0, tail[h, 0:6], tail[h, 6:12])[:, 0:32])
    grad_ref[:, 0:128] = grads[0]
    grad_ref[:, 128:160] = grads[1]
    grad_ref[:, 160:288] = grads[2]
    grad_ref[:, 288:320] = grads[3]
    for copy in pending:
        copy.wait_send()


def hand_out(loss_in, grad_in, loss_ref, grad_ref, sem):
    copies = [
        pltpu.make_async_copy(loss_in, loss_ref, sem.at[0]),
        pltpu.make_async_copy(grad_in, grad_ref, sem.at[1]),
    ]
    for copy in copies:
        copy.start()
    for copy in copies:
        copy.wait()


def on_device(
    student_hidden, teacher_hidden, student_head, teacher_head,
    teacher_row, live_counts, branch_id, branch_ratio,
):
    vmem = pl.BlockSpec(memory_space=pltpu.VMEM)
    hbm = pl.BlockSpec(memory_space=pl.ANY)
    loss, grad = pl.pallas_call(
        kernel,
        out_shape=(
            jax.ShapeDtypeStruct((1, 6), F32),
            jax.ShapeDtypeStruct((6, 320), F32),
        ),
        in_specs=[hbm] * 8,
        out_specs=(vmem, vmem),
        scratch_shapes=[
            pltpu.VMEM((6, 320), BF16),
            pltpu.VMEM((6, 256), BF16),
            pltpu.VMEM((1, 192), jnp.int32),
            pltpu.VMEM((1, 32), jnp.int32),
            pltpu.VMEM((1, 192), jnp.int32),
            pltpu.VMEM((1, 16), F32),
            pltpu.VMEM((280, 5120), BF16),
            pltpu.VMEM((280, 4096), BF16),
            pltpu.VMEM((2, 16, 160, 280), BF16),
            pltpu.VMEM((16, 160, 280), BF16),
            pltpu.VMEM((8, 384), F32),
            pltpu.VMEM((2, 16, 128), BF16),
            pltpu.VMEM((16, 2, 16, 128), BF16),
            pltpu.VMEM((3, LIVE, 512), BF16),
            pltpu.VMEM((2, 16, HALF, 128), BF16),
            pltpu.VMEM((256, 640), BF16),
            pltpu.VMEM((2, 8, 128), F32),
            pltpu.VMEM((16, 8, 128), F32),
            pltpu.VMEM((16, 8, 128), F32),
            pltpu.VMEM((2, 288, 256), BF16),
            pltpu.VMEM((3, 4, 160, 256), BF16),
            pltpu.VMEM((3, 4, 160, 256), BF16),
            pltpu.VMEM((4, 160, 256), F32),
            pltpu.VMEM((3, 160, 128), BF16),
            pltpu.VMEM((3, 160, 128), BF16),
            pltpu.VMEM((128, 640), BF16),
            pltpu.VMEM((16, 16, 128), BF16),
            pltpu.VMEM((16, 16, 128), BF16),
            pltpu.VMEM((2, 16, 128), F32),
            pltpu.VMEM((2, 16, 128), F32),
            pltpu.SemaphoreType.DMA((2,)),
            pltpu.SemaphoreType.DMA((6,)),
            pltpu.SemaphoreType.DMA((N_SEMS,)),
            pltpu.SemaphoreType.DMA((N_SEMS,)),
        ],
        compiler_params=pltpu.CompilerParams(
            collective_id=0, has_side_effects=True, vmem_limit_bytes=60 * 1024 * 1024
        ),
    )(
        student_hidden, teacher_hidden, student_head.T, teacher_head.T,
        teacher_row.reshape(1, -1), live_counts.reshape(1, -1),
        branch_id.reshape(1, -1), branch_ratio.reshape(1, -1),
    )
    loss, grad = pl.pallas_call(
        hand_out,
        out_shape=(
            jax.ShapeDtypeStruct((1, 6), F32),
            jax.ShapeDtypeStruct((6, 320), F32),
        ),
        in_specs=[hbm, hbm],
        out_specs=(hbm, hbm),
        scratch_shapes=[pltpu.SemaphoreType.DMA((2,))],
        compiler_params=pltpu.CompilerParams(vmem_limit_bytes=60 * 1024 * 1024),
    )(loss, grad)
    return loss.reshape(6), grad


def solution(mesh):
    in_specs = (
        P("rows", "vocab"),
        P("rows", "vocab"),
        P(None, ("rows", "vocab")),
        P(None, ("rows", "vocab")),
        P(),
        P(),
        P(),
        P(),
    )
    out_specs = (P("rows"), P("rows", "vocab"))
    return jax.shard_map(
        on_device, mesh=mesh, in_specs=in_specs,
        out_specs=out_specs, check_vma=False,
    )
```

```python
import jax
import jax.numpy as jnp
from jax import lax
from jax.experimental import pallas as pl
from jax.experimental.pallas import tpu as pltpu
from jax.sharding import PartitionSpec as P

MESH = pl.DeviceIdType.MESH
F32 = jnp.float32
BF16 = jnp.bfloat16
LIVE = 112
HALF = 256

SIB_P, SIB_X, SIB_ST, SIB_W, SIB_G, SIB_R5 = 0, 1, 17, 18, 20, 21
ZP, ZST, ZR = 22, 37, 52
PA, PB, PST, R2, R3 = 67, 70, 82, 97, 100
N_SEMS = 103
Z_ORDER = (8, 7, 9, 6, 10, 5, 11, 4, 12, 3, 13, 2, 14, 1, 15)


def iota(shape, dim):
    return lax.broadcasted_iota(jnp.int32, shape, dim)


def sixth(n):
    return lax.shift_right_logical(n * 171, 10)


def as_col(row, n):
    eye = iota((n, n), 0) == iota((n, n), 1)
    return jnp.sum(jnp.where(eye, row, 0.0), axis=1, keepdims=True)


def as_row(col, n):
    eye = iota((n, n), 0) == iota((n, n), 1)
    return jnp.sum(jnp.where(eye, col, 0.0), axis=0, keepdims=True)


def merge(stats):
    part = [stats[:, k, :] for k in range(5)]
    peak_s = jnp.max(part[0], axis=0, keepdims=True)
    peak_t = jnp.max(part[1], axis=0, keepdims=True)
    scale_s = jnp.exp(part[0] - peak_s)
    scale_t = jnp.exp(part[1] - peak_t)
    sum_s = jnp.sum(scale_s * part[2], axis=0, keepdims=True)
    sum_t = jnp.sum(scale_t * part[3], axis=0, keepdims=True)
    cross = jnp.sum(scale_s * part[4], axis=0, keepdims=True)
    return peak_s, peak_t, sum_s, sum_t, cross


def put_stats(ref, parts):
    row = iota((8, 128), 0)
    out = jnp.zeros((8, 128), F32)
    for k, part in enumerate(parts):
        out = jnp.where(row == k, part, out)
    ref[...] = out


def kernel(
    sh_hbm, th_hbm, ws_hbm, wt_hbm, trow_hbm, live_hbm, branch_hbm, ratio_hbm,
    loss_ref, grad_ref,
    sh_ref, th_ref, trow_ref, live_ref, branch_ref, ratio_ref,
    wst, wtt, wh, wsib, wide, parts, zbuf, sel, xbuf, un, st_a, st_b, st_c,
    g2, sb2, rb2, acc2, sb3, rb3, place, sb4, rb4, sb5, tail,
    head_sem, small_sem, send, recv,
):
    r = lax.axis_index("rows")
    v = lax.axis_index("vocab")
    z = lax.div(r, 2)
    c = lax.rem(r, 2)
    x = lax.div(v, 4)
    y = lax.rem(v, 4)
    o = 1 - c
    a = x * o + y * c
    b = y * o + x * c

    def v_of(pa, pb):
        return (pa * 4 + pb) * o + (pb * 4 + pa) * c

    def v_sib(pa, pb):
        return (pa * 4 + pb) * c + (pb * 4 + pa) * o

    sibling = (z * 2 + o, v)

    def z_dev(d):
        return (lax.rem(z + d, 16) * 2 + c, v)

    def plane_dev(da, db):
        return (r, v_of(lax.rem(a + da, 4), lax.rem(b + db, 4)))

    def rcopy(src, dst, number, device):
        return pltpu.make_async_remote_copy(
            src_ref=src, dst_ref=dst, send_sem=send.at[number], recv_sem=recv.at[number],
            device_id=device, device_id_type=MESH,
        )

    pending = []

    def go(src, dst, number, device):
        copy = rcopy(src, dst, number, device)
        copy.start()
        pending.append(copy)

    def arrive(dst, number):
        rcopy(dst, dst, number, sibling).wait_recv()

    heads = [
        pltpu.make_async_copy(ws_hbm, wst, head_sem.at[0]),
        pltpu.make_async_copy(wt_hbm, wtt, head_sem.at[1]),
    ]
    small = [
        pltpu.make_async_copy(src, dst, small_sem.at[n])
        for n, (src, dst) in enumerate((
            (sh_hbm, sh_ref), (th_hbm, th_ref), (trow_hbm, trow_ref),
            (live_hbm, live_ref), (branch_hbm, branch_ref), (ratio_hbm, ratio_ref),
        ))
    ]
    for copy in small + heads:
        copy.start()

    plane = [(da, db) for da in range(4) for db in range(4) if (da, db) != (0, 0)]
    plane.sort(key=lambda at: -min(at[0], 4 - at[0]) - min(at[1], 4 - at[1]))
    barrier = pltpu.get_barrier_semaphore()
    for d in Z_ORDER:
        pl.semaphore_signal(barrier, inc=1, device_id=z_dev(d), device_id_type=MESH)
    for da, db in plane:
        pl.semaphore_signal(barrier, inc=1, device_id=plane_dev(da, db), device_id_type=MESH)
    pl.semaphore_signal(barrier, inc=1, device_id=sibling, device_id_type=MESH)
    for copy in small:
        copy.wait()

    row16 = iota((16, 128), 0)
    wide[...] = jnp.zeros_like(wide)
    wide[0:6, 0:320] = sh_ref[...].astype(F32)
    sw = wide[...]
    odd = lax.rem(v, 2) == 1
    sw_odd = jnp.concatenate([pltpu.roll(sw, 320, 1)[:, 0:256], sw[:, 0:128]], axis=1)
    sw = jnp.where(odd, sw_odd, sw)
    s2 = jnp.where(iota((8, 128), 1) < 64, sw[:, 256:384], 0.0)
    s2_high = pltpu.roll(s2, 64, 1)
    th = th_ref[...].astype(F32)
    pack_s = jnp.zeros((16, 128), F32)
    pack_t = jnp.zeros((16, 128), F32)
    for i in range(6):
        pack_s = jnp.where(row16 == i, sw[i:i + 1, 0:128], pack_s)
        pack_s = jnp.where(row16 == 6 + i, sw[i:i + 1, 128:256], pack_s)
        pack_t = jnp.where(row16 == i, th[i:i + 1, 0:128], pack_t)
        pack_t = jnp.where(row16 == 6 + i, th[i:i + 1, 128:256], pack_t)
    for i in range(3):
        both = s2[i:i + 1, :] + s2_high[i + 3:i + 4, :]
        pack_s = jnp.where(row16 == 12 + i, both, pack_s)
        pack_t = jnp.where(row16 == 12 + i, both, pack_t)
    parts[0] = pack_s.astype(BF16)
    parts[1] = pack_t.astype(BF16)
    zbuf[z, c] = parts[c]

    live_row = live_ref[...].astype(F32)
    live_col = as_col(live_row, 32)
    owner_a, owner_b = iota((32, 32), 0), iota((32, 32), 1)
    before_col = jnp.sum(jnp.where(owner_b < owner_a, live_row, 0.0), axis=1, keepdims=True)
    before_row = jnp.sum(jnp.where(owner_a < owner_b, live_col, 0.0), axis=0, keepdims=True)
    pos = iota((1, 192), 1)
    pos_owner = sixth(pos)
    pos_slot = (pos - 6 * pos_owner).astype(F32)
    own = iota((32, 192), 0) == sixth(iota((32, 192), 1))
    rank = jnp.sum(jnp.where(own, before_col, 0.0), axis=0, keepdims=True) + pos_slot
    alive = jnp.sum(jnp.where(own, live_col, 0.0), axis=0, keepdims=True) > pos_slot
    rank = jnp.where(alive, rank, -1.0).astype(jnp.int32)
    pick = iota((128, 192), 0) == rank
    pos_of = jnp.sum(jnp.where(pick, pos.astype(F32), 0.0), axis=1, keepdims=True)
    teacher_of = jnp.sum(jnp.where(pick, trow_ref[...].astype(F32), 0.0), axis=1, keepdims=True)
    ratio_col = as_col(ratio_ref[...], 16)
    ratio_of = jnp.sum(
        jnp.where(iota((16, 192), 0) == branch_ref[...], ratio_col, 0.0), axis=0, keepdims=True
    )
    weight = as_row(jnp.sum(jnp.where(pick, ratio_of, 0.0), axis=1, keepdims=True), 128)
    def origin(source):
        owner = sixth(source)
        at_z = lax.shift_right_logical(owner, 1)
        return at_z * 32 + jnp.bitwise_and(owner, 1) * 16, source - 6 * owner

    pos_of = pos_of.astype(jnp.int32)[0:LIVE]
    base, src_slot = origin(jnp.where(c == 0, pos_of, teacher_of.astype(jnp.int32)[0:LIVE]))
    base_s, slot_s = origin(pos_of)
    low = slot_s < 3
    column = iota((LIVE, 512), 1)
    for k, at in enumerate((
        base + src_slot, base + 6 + src_slot, base_s + 12 + jnp.where(low, slot_s, slot_s - 3)
    )):
        sel[k] = jnp.where(column == at, 1.0, 0.0).astype(BF16)

    dest = iota((256, 1), 0)
    dest_z, q = lax.shift_right_logical(dest, 4), jnp.bitwise_and(dest, 15)

    def back(row, wanted):
        second = jnp.where(row >= 6, 1, 0)
        owner = 2 * dest_z + second
        slot = (row - 6 * second).astype(F32)
        mine = iota((256, 32), 1) == owner
        start = jnp.sum(jnp.where(mine, before_row, 0.0), axis=1, keepdims=True)
        count = jnp.sum(jnp.where(mine, live_row, 0.0), axis=1, keepdims=True)
        j = jnp.where(wanted & (slot < count), start + slot, -1.0).astype(jnp.int32)
        return jnp.where(iota((256, 128), 1) == j, 1.0, 0.0).astype(BF16)

    place[...] = jnp.zeros_like(place)
    un[:, 0:128] = back(q, q < 12)
    for g in range(4):
        un[:, 128 * g + 128:128 * g + 256] = back((q - 12) * 4 + g, (q >= 12) & (q < 15))

    pl.semaphore_wait(barrier, 31)
    go(parts.at[o], zbuf.at[z, c], SIB_P, sibling)
    arrive(zbuf.at[z, o], SIB_P)
    for n, d in enumerate(Z_ORDER):
        go(zbuf.at[z], zbuf.at[z], ZP + n, z_dev(d))

    def turn(part):
        for u in range(4 * part, 4 * part + 4):
            turned = jnp.transpose(wst[:, 640 * u:640 * u + 640])
            for k in range(4):
                wh[k % 2, 2 * u + k // 2] = turned[160 * k:160 * k + 160]
        where = pl.ds(8 * part, 8)
        go(wh.at[o, where], wsib.at[where], SIB_W + part, sibling)

    heads[0].wait()
    turn(0)
    for n, d in enumerate(Z_ORDER):
        arrive(zbuf.at[lax.rem(z + 16 - d, 16)], ZP + n)
    raw = zbuf[...].reshape(512, 128)
    chunk = [jnp.dot(sel[k], raw, preferred_element_type=F32) for k in range(3)]
    turned = pltpu.roll(chunk[2], 64, 1)
    lane = iota((64, 128), 1)
    in_low, in_high = jnp.where(low, chunk[2], turned), jnp.where(low, turned, chunk[2])
    packed = jnp.where(
        odd,
        jnp.where(lane < 64, in_low[48:112], in_high[0:64]),
        jnp.where(lane < 64, in_low[0:64], in_high[48:112]),
    )
    xbuf[c, v, 0:112] = chunk[0].astype(BF16)
    xbuf[c, v, 112:224] = chunk[1].astype(BF16)
    xbuf[c, v, 224:256] = jnp.where(c == 0, packed[0:32], packed[32:64]).astype(BF16)

    def spread(pa, n):
        block = xbuf.at[c, v_of(pa, b)]
        for k, d in enumerate((2, 1, 3)):
            go(block, block, PB + 3 * n + k, plane_dev(0, d))
        go(block, block, SIB_X + n, sibling)

    mine = xbuf.at[c, v]
    for k, d in enumerate((1, 3, 2)):
        go(mine, mine, PA + k, plane_dev(d, 0))
    spread(a, 0)
    turn(1)
    for k, d in enumerate((1, 3, 2)):
        pa = lax.rem(a + 4 - d, 4)
        arrive(xbuf.at[c, v_of(pa, b)], PA + k)
        spread(pa, k + 1)
    heads[1].wait()
    nt = (((1,), (1,)), ((), ()))
    student = jnp.zeros((280, LIVE), F32)
    teacher = jnp.zeros((280, LIVE), F32)

    def rows_of(part, w):
        return jnp.concatenate([xbuf[part, w, 0:112], xbuf[part, w, 112:224]], axis=1)

    def come(n, d0):
        for k, d in enumerate((2, 1, 3)):
            block = xbuf.at[c, v_of(lax.rem(a + 4 - d0, 4), lax.rem(b + 4 - d, 4))]
            arrive(block, PB + 3 * n + k)
            go(block, block, SIB_X + 4 + 3 * n + k, sibling)

    def come_over(n, d0):
        pa = lax.rem(b + 4 - d0, 4)
        arrive(xbuf.at[o, v_sib(pa, a)], SIB_X + n)
        for k, d in enumerate((2, 1, 3)):
            arrive(xbuf.at[o, v_sib(pa, lax.rem(a + 4 - d, 4))], SIB_X + 4 + 3 * n + k)

    def logits_of(student, teacher, d0):
        at = lax.rem(x + 4 - d0, 4)
        left = [
            wst[:, pl.ds(pl.multiple_of(1280 * at + begin, 128), 256)] for begin in (0, 384, 640, 1024)
        ]
        right = [rows_of(0, 4 * at + k) for k in range(4)]
        student += lax.dot_general(
            jnp.concatenate(left, axis=1), jnp.concatenate(right, axis=1), nt,
            preferred_element_type=F32,
        )
        at = lax.rem(y + 4 - d0, 4)
        left = [wtt[:, pl.ds(pl.multiple_of(1024 * k + 256 * at, 128), 256)] for k in range(4)]
        right = [rows_of(1, 4 * k + at) for k in range(4)]
        teacher += lax.dot_general(
            jnp.concatenate(left, axis=1), jnp.concatenate(right, axis=1), nt,
            preferred_element_type=F32,
        )
        return student, teacher

    places = (0, 1, 3, 2)
    for n, d0 in enumerate(places):
        come(n, d0)
        if n:
            come_over(n - 1, places[n - 1])
            student, teacher = logits_of(student, teacher, places[n - 1])
    come_over(3, places[3])
    for part in range(2):
        where = pl.ds(8 * part, 8)
        arrive(wsib.at[where], SIB_W + part)
    student, teacher = logits_of(student, teacher, places[3])
    lane = iota((64, 128), 1)
    for part in range(2):
        left, right = [], []
        for u in range(4 * part, 4 * part + 4):
            first, second = [
                jnp.concatenate([xbuf[0, w, 224:256], xbuf[1, w, 224:256]], axis=0).astype(F32)
                for w in (2 * u, 2 * u + 1)
            ]
            top = jnp.where(lane < 64, first, second)
            rest = pltpu.roll(jnp.where(lane < 64, second, first), 64, 1)[16:64]
            left.append(wst[:, 640 * u + 256:640 * u + 384])
            right.append(jnp.concatenate([top, rest], axis=0).astype(BF16))
        student += lax.dot_general(
            jnp.concatenate(left, axis=1), jnp.concatenate(right, axis=1), nt,
            preferred_element_type=F32,
        )
    zeros = jnp.zeros((280, 128 - LIVE), F32)
    student = jnp.concatenate([student, zeros], axis=1)
    teacher = jnp.concatenate([teacher, zeros], axis=1)
    diff = student - teacher
    peak_s = jnp.max(student, axis=0, keepdims=True)
    peak_t = jnp.max(teacher, axis=0, keepdims=True)
    expo = jnp.exp(student - peak_s)
    put_stats(st_a.at[c], (
        peak_s, peak_t,
        jnp.sum(expo, axis=0, keepdims=True),
        jnp.sum(jnp.exp(teacher - peak_t), axis=0, keepdims=True),
        jnp.sum(expo * diff, axis=0, keepdims=True),
    ))

    go(st_a.at[c], st_a.at[c], SIB_ST, sibling)
    arrive(st_a.at[o], SIB_ST)
    chip = merge(st_a[...])
    mass = expo * jnp.exp(peak_s - chip[0])
    g2[c, 272:288] = jnp.zeros((16, 256), BF16)
    g2[c, 0:280, 0:128] = (mass * (diff - chip[4] / chip[2])).astype(BF16)
    g2[c, 0:280, 128:256] = mass.astype(BF16)
    go(g2.at[c], g2.at[c], SIB_G, sibling)
    put_stats(st_b.at[v], chip)
    for n, (da, db) in enumerate(plane):
        go(st_b.at[v], st_b.at[v], PST + n, plane_dev(da, db))
    arrive(g2.at[o], SIB_G)

    def products(d):
        places_here = [v_of(pa, lax.rem(b + d, 4)) for pa in range(4)]
        total = jnp.dot(
            jnp.concatenate([wh[c, w] for w in places_here], axis=0), g2[c, 0:280],
            preferred_element_type=F32,
        )
        total += jnp.dot(
            jnp.concatenate([wsib[w] for w in places_here], axis=0), g2[o, 0:280],
            preferred_element_type=F32,
        )
        if d:
            sb2[d - 1] = total.astype(BF16).reshape(4, 160, 256)
        else:
            acc2[...] = total.reshape(4, 160, 256)

    for d in (2, 1, 3):
        products(d)
        go(sb2.at[d - 1], rb2.at[d - 1], R2 + d - 1, plane_dev(0, d))
    for n, (da, db) in enumerate(plane):
        arrive(st_b.at[v_of(lax.rem(a + 4 - da, 4), lax.rem(b + 4 - db, 4))], PST + n)
    put_stats(st_c.at[z], merge(st_b[...]))
    for n, d in enumerate(Z_ORDER):
        go(st_c.at[z], st_c.at[z], ZST + n, z_dev(d))
    products(0)
    for d in (1, 3, 2):
        arrive(rb2.at[d - 1], R2 + d - 1)
    for n, d in enumerate(Z_ORDER):
        arrive(st_c.at[lax.rem(z + 16 - d, 16)], ZST + n)
    peak_s, peak_t, sum_s, sum_t, cross = merge(st_c[...])
    lse_s = peak_s + jnp.log(sum_s)
    lse_t = peak_t + jnp.log(sum_t)
    divergence = cross / sum_s - lse_s + lse_t
    loss = as_col(weight * divergence, 128)
    ours = iota((1, 32), 1) == r
    start = jnp.sum(jnp.where(ours, before_row, 0.0), axis=1, keepdims=True)
    count = jnp.sum(jnp.where(ours, live_row, 0.0), axis=1, keepdims=True)
    slot = iota((1, 128), 1).astype(F32)
    at = jnp.where(slot < count, start + slot, -1.0).astype(jnp.int32)
    loss_ref[...] = jnp.sum(
        jnp.where(iota((128, 128), 0) == at, loss, 0.0), axis=0, keepdims=True
    )[:, 0:6]
    mean = cross / sum_s
    scales, shifts = [], []
    for d in range(4):
        shard = st_b[v_of(a, lax.rem(b + 4 - d, 4))]
        scales.append(weight * jnp.exp(shard[0:1] - peak_s) / sum_s)
        shifts.append(shard[4:5] / shard[2:3] - mean)
    for d in (2, 1, 3, 0):
        pa = lax.rem(a + d, 4)
        term = acc2[pa]
        total = scales[0] * (term[:, 0:128] + shifts[0] * term[:, 128:256])
        for k in range(3):
            term = rb2[k, pa].astype(F32)
            total += scales[k + 1] * (term[:, 0:128] + shifts[k + 1] * term[:, 128:256])
        if d:
            sb3[d - 1] = total.astype(BF16)
            go(sb3.at[d - 1], rb3.at[d - 1], R3 + d - 1, plane_dev(d, 0))
    for d in (1, 3, 2):
        arrive(rb3.at[d - 1], R3 + d - 1)
        total += rb3[d - 1].astype(F32)
    total = total.astype(BF16)

    place[:, 0:128] = total[0:128]
    for k in range(4):
        place[32 * k:32 * k + 32, 128 * k + 128:128 * k + 256] = total[128:160]
    spread_out = lax.dot_general(un[...], place[...], nt, preferred_element_type=F32)
    sb4[...] = spread_out.astype(BF16).reshape(16, 16, 128)
    rb4[z] = sb4[z]
    for n, d in enumerate(Z_ORDER):
        go(sb4.at[lax.rem(z + d, 16)], rb4.at[z], ZR + n, z_dev(d))
    for n, d in enumerate(Z_ORDER):
        arrive(rb4.at[lax.rem(z + 16 - d, 16)], ZR + n)
    full = jnp.sum(rb4[...].astype(F32), axis=0)
    sb5[c] = full
    go(sb5.at[c], sb5.at[c], SIB_R5, sibling)

    def ends(h, block):
        for row in range(12):
            at = 32 * (row % 4)
            tail[h, row:row + 1, 0:32] = block[12 + row // 4:13 + row // 4, at:at + 32]

    ends(c, full)
    arrive(sb5.at[o], SIB_R5)
    ends(o, sb5[o])
    grads = []
    for h in range(2):
        block = sb5[h]
        grads.append(jnp.where(c == 0, block[0:6], block[6:12]))
        grads.append(jnp.where(c == 0, tail[h, 0:6], tail[h, 6:12])[:, 0:32])
    grad_ref[:, 0:128] = grads[0]
    grad_ref[:, 128:160] = grads[1]
    grad_ref[:, 160:288] = grads[2]
    grad_ref[:, 288:320] = grads[3]
    for copy in pending:
        copy.wait_send()


def hand_out(loss_in, grad_in, loss_ref, grad_ref, sem):
    copies = [
        pltpu.make_async_copy(loss_in, loss_ref, sem.at[0]),
        pltpu.make_async_copy(grad_in, grad_ref, sem.at[1]),
    ]
    for copy in copies:
        copy.start()
    for copy in copies:
        copy.wait()


def on_device(
    student_hidden, teacher_hidden, student_head, teacher_head,
    teacher_row, live_counts, branch_id, branch_ratio,
):
    vmem = pl.BlockSpec(memory_space=pltpu.VMEM)
    hbm = pl.BlockSpec(memory_space=pl.ANY)
    loss, grad = pl.pallas_call(
        kernel,
        out_shape=(
            jax.ShapeDtypeStruct((1, 6), F32),
            jax.ShapeDtypeStruct((6, 320), F32),
        ),
        in_specs=[hbm] * 8,
        out_specs=(vmem, vmem),
        scratch_shapes=[
            pltpu.VMEM((6, 320), BF16),
            pltpu.VMEM((6, 256), BF16),
            pltpu.VMEM((1, 192), jnp.int32),
            pltpu.VMEM((1, 32), jnp.int32),
            pltpu.VMEM((1, 192), jnp.int32),
            pltpu.VMEM((1, 16), F32),
            pltpu.VMEM((280, 5120), BF16),
            pltpu.VMEM((280, 4096), BF16),
            pltpu.VMEM((2, 16, 160, 280), BF16),
            pltpu.VMEM((16, 160, 280), BF16),
            pltpu.VMEM((8, 384), F32),
            pltpu.VMEM((2, 16, 128), BF16),
            pltpu.VMEM((16, 2, 16, 128), BF16),
            pltpu.VMEM((3, LIVE, 512), BF16),
            pltpu.VMEM((2, 16, HALF, 128), BF16),
            pltpu.VMEM((256, 640), BF16),
            pltpu.VMEM((2, 8, 128), F32),
            pltpu.VMEM((16, 8, 128), F32),
            pltpu.VMEM((16, 8, 128), F32),
            pltpu.VMEM((2, 288, 256), BF16),
            pltpu.VMEM((3, 4, 160, 256), BF16),
            pltpu.VMEM((3, 4, 160, 256), BF16),
            pltpu.VMEM((4, 160, 256), F32),
            pltpu.VMEM((3, 160, 128), BF16),
            pltpu.VMEM((3, 160, 128), BF16),
            pltpu.VMEM((128, 640), BF16),
            pltpu.VMEM((16, 16, 128), BF16),
            pltpu.VMEM((16, 16, 128), BF16),
            pltpu.VMEM((2, 16, 128), F32),
            pltpu.VMEM((2, 16, 128), F32),
            pltpu.SemaphoreType.DMA((2,)),
            pltpu.SemaphoreType.DMA((6,)),
            pltpu.SemaphoreType.DMA((N_SEMS,)),
            pltpu.SemaphoreType.DMA((N_SEMS,)),
        ],
        compiler_params=pltpu.CompilerParams(
            collective_id=0, has_side_effects=True, vmem_limit_bytes=60 * 1024 * 1024
        ),
    )(
        student_hidden, teacher_hidden, student_head.T, teacher_head.T,
        teacher_row.reshape(1, -1), live_counts.reshape(1, -1),
        branch_id.reshape(1, -1), branch_ratio.reshape(1, -1),
    )
    loss, grad = pl.pallas_call(
        hand_out,
        out_shape=(
            jax.ShapeDtypeStruct((1, 6), F32),
            jax.ShapeDtypeStruct((6, 320), F32),
        ),
        in_specs=[hbm, hbm],
        out_specs=(hbm, hbm),
        scratch_shapes=[pltpu.SemaphoreType.DMA((2,))],
        compiler_params=pltpu.CompilerParams(vmem_limit_bytes=60 * 1024 * 1024),
    )(loss, grad)
    return loss.reshape(6), grad


def solution(mesh):
    in_specs = (
        P("rows", "vocab"),
        P("rows", "vocab"),
        P(None, ("rows", "vocab")),
        P(None, ("rows", "vocab")),
        P(),
        P(),
        P(),
        P(),
    )
    out_specs = (P("rows"), P("rows", "vocab"))
    return jax.shard_map(
        on_device, mesh=mesh, in_specs=in_specs,
        out_specs=out_specs, check_vma=False,
    )
```
